32 devices in a mesh: dp: 2 (over core), fsdp: 4 (over z), tp: 4 (over y, x).
Axes of the slice: x: 2, y: 2, z: 4, core: 2. Of those that a mesh axis runs over, the one named last changes fastest.
Arguments:
- layer_input: bfloat16 [4096, 4096], P(('dp', 'fsdp'), 'tp'), may hold values from -6 to 6
- value_grad: bfloat16 [4096, 2048], P(('dp', 'fsdp'), 'tp'), may hold values from -6 to 6
- residual_grad: bfloat16 [4096, 4096], P(('dp', 'fsdp'), 'tp'), may hold values from -6 to 6
- value_weight: bfloat16 [4096, 2048], P(('tp', 'fsdp')), may hold values from -0.125 to 0.125
- owner: int32 [4096, 1], P(('dp', 'fsdp')), may hold values from 0 to 3; in each aligned block of 512 rows (0 to 511, 512 to 1023, ...) at most 256 rows name the same one
- key_row: int32 [4096], P(('dp', 'fsdp')), may hold values from 0 to 255
Outputs:
- weight_grad: float32 [4096, 2048], P(('tp', 'fsdp'))
- key_grad: float32 [1024, 4096], P('fsdp', 'tp')
The draws below stay inside these ranges and needn't reach their ends.
Inputs may be any that keep to these rules, and one draw needn't show every extreme that they name: Among the 512 tokens of one device (aligned blocks of rows) at most 256 name the same owner, and that bound is reached.
All inputs are finite; a program needn't handle non-finite values.
Results may differ from the reference program's by a relative error of at most 0.0029.
Values may be sent and summed in bfloat16 or wider, within the bound.
No kernel may reach another device: no remote copies, remote signals or barrier semaphores. Data moves between devices by JAX's collectives and lax.ppermute only.
A program may use at most 64 MiB of HBM per device.

```python
import math
import jax
import jax.numpy as jnp
import numpy as np
from jax import lax

D = 4096
HW = 2048
TOK_DEV = 512
KEY_DEV = 256
CAP = 256
TOKENS = 4096
NKEYS = 1024
N_FSDP = 4


def place_ends(drawn, rng, smallest, largest):
    longest = drawn.shape.index(max(drawn.shape))
    spots = []
    for shift in (0, 1):
        where = [jax.random.randint(jax.random.fold_in(rng, axis), (), 0, length) for axis, length in enumerate(drawn.shape)]
        where[longest] = (where[longest] + shift) % drawn.shape[longest]
        spots.append(tuple(where))
    return drawn.at[spots[0]].set(smallest).at[spots[1]].set(largest)


def with_spikes(array, stream_key, source, target, shards_of, factor):
    owner, partner = [(jnp.arange(array.shape[axis_at]) // (array.shape[axis_at] // shards_of)).reshape([-1 if axis == axis_at else 1 for axis in range(array.ndim)]) for axis_at in (source, target)]
    chosen = jax.random.permutation(stream_key, shards_of)[partner]
    strong = (owner == chosen) | (owner == (partner + shards_of // 2) % shards_of)
    return jnp.where(strong, factor * array, array)


def block_levels(rng, shape, shards, least, largest):
    def one(position, shards_of):
        draws = jax.random.uniform(jax.random.fold_in(jax.random.fold_in(rng, 6), position), (shards_of,), jnp.float32, least / len(shards), largest / len(shards))
        return jnp.repeat(jnp.exp(draws), shape[position] // shards_of).reshape((-1,) + (1,) * (len(shape) - position - 1))

    level = one(*shards[0])
    for cut in shards[1:]:
        level = level * one(*cut)
    return level


def deal_out(key, own, number, rows, count, top, bound, lean):
    ranking = jax.random.permutation(key, count)
    heavy_load, common = shares(count, rows * top, bound, lean, True), shares(count, rows * top, bound, lean, False)
    places = jnp.arange(count)

    def named(tallies, offset_by):
        used = int((tallies > 0).sum())
        fixed = max(1, used // 4)
        passed = fixed + (places - fixed + offset_by * (used - fixed)) % max(1, count - fixed)
        return jnp.zeros((count,), jnp.int32).at[ranking[jnp.where(places < fixed, places, passed)]].set(jnp.asarray(tallies, jnp.int32))

    tallies = jnp.where(number % 4 == 0, named(heavy_load, number // 4), named(common, number - number // 4 - 1))
    mixed = jax.random.permutation(jax.random.fold_in(own, 3), count)
    giver, taker = mixed[0:count // 2 * 2:2], mixed[1:count // 2 * 2:2]
    margin = jnp.minimum(tallies[giver] - 1, bound - tallies[taker]) // 2
    margin = jnp.where((giver == ranking[0]) | (taker == ranking[0]) | (tallies[taker] == 0), 0, jnp.maximum(margin, 0))
    passed = jax.random.randint(jax.random.fold_in(own, 4), (count // 2,), 0, 1 << 20) % (margin + 1)
    tallies = tallies.at[giver].add(-passed).at[taker].add(passed)
    labels = jnp.searchsorted(jnp.cumsum(tallies), jnp.arange(rows * top), side="right").astype(jnp.int32)
    grid = labels.reshape(top, rows).T
    grid = grid[jax.random.permutation(jax.random.fold_in(own, 1), rows)]
    offset_by = jax.random.randint(jax.random.fold_in(own, 2), (rows, 1), 0, top)
    return jnp.take_along_axis(grid, (jnp.arange(top)[None, :] + offset_by) % top, axis=1)


def shares(amount, total, most, slope, full):
    loads = [(1 << 20) // math.isqrt(grade ** slope) + 1 for grade in range(1, amount + 1)]
    largest = most if full else min(most, max(-(-total // amount), total * loads[0] // sum(loads)))
    least = 1 if total - largest >= amount - 1 else 0
    holding, surplus = [largest] + [least] * (amount - 1), total - largest - least * (amount - 1)
    while surplus > 0:
        movable = [i for i in range(1, amount) if holding[i] < largest] or [i for i in range(1, amount) if holding[i] < most]
        pool, remaining = sum([loads[i] for i in movable]), surplus
        for i in movable:
            extra = min(most - holding[i], max(1, remaining * loads[i] // pool), surplus)
            holding[i] = holding[i] + extra
            surplus = surplus - extra
    return np.array(holding)


def gaussian(own_key, dims, scale, reach, pieces=(), held_as=jnp.bfloat16):
    array = jax.random.normal(own_key, dims, jnp.float32) * scale
    if len(pieces) > 0:
        array = block_levels(own_key, dims, pieces, -0.22, 0.18) * array
    return jnp.clip(array, min=-reach, max=reach).astype(held_as)


def noise_with(rng, extent, width, limit, split, heavy, dtype=jnp.bfloat16):
    result = width * jax.random.normal(rng, extent, jnp.float32)
    if split:
        result = result * block_levels(rng, extent, split, -0.22, 0.18)
    return jnp.clip(with_spikes(result, jax.random.fold_in(rng, 3), *heavy), -limit, limit).astype(dtype)


def setup_inputs(seed: int = 0) -> dict:
    seeds = jax.random.split(jax.random.key(seed), 7)
    layer_input = noise_with(seeds[0], (TOKENS, D), 1.0, 6.0, ((0, 8), (1, 4)), (0, 1, 8, 2.0))
    value_grad = gaussian(seeds[1], (TOKENS, HW), 1.0, 6.0, ((0, 8), (1, 4)))
    residual_grad = gaussian(seeds[2], (TOKENS, D), 1.0, 6.0, ((0, 8), (1, 4)))
    value_weight = gaussian(seeds[3], (D, HW), HW ** -0.5, 0.125, ((0, 16),))
    owner_keys = jax.random.split(jax.random.fold_in(seeds[4], 1), TOKENS // TOK_DEV)
    owner_turns = jax.random.permutation(jax.random.fold_in(seeds[4], 3), TOKENS // TOK_DEV)
    owner = jax.vmap(lambda own, number: deal_out(jax.random.fold_in(seeds[4], 2), own, number, TOK_DEV, N_FSDP, 1, CAP, 2))(owner_keys, owner_turns).reshape((TOKENS, 1))
    key_row = place_ends(jax.random.randint(seeds[5], (TOKENS,), 0, KEY_DEV), jax.random.fold_in(seeds[5], 1), 0, KEY_DEV - 1).astype(jnp.int32)
    return dict(layer_input=layer_input, value_grad=value_grad, residual_grad=residual_grad, value_weight=value_weight, owner=owner, key_row=key_row)


def reference(layer_input, value_grad, residual_grad, value_weight, owner, key_row):
    blocks = TOKENS // TOK_DEV
    inputs = layer_input.reshape(blocks, TOK_DEV, D)
    grads = value_grad.reshape(blocks, TOK_DEV, HW)
    residual = residual_grad.reshape(blocks, TOK_DEV, D)
    keys = (owner[:, 0] * KEY_DEV + key_row).astype(jnp.int32).reshape(blocks, TOK_DEV)

    def step(carry, items):
        weight_acc, table = carry
        block_in, block_grad, block_res, block_keys = items
        partial_value = jnp.dot(block_in.T, block_grad, preferred_element_type=jnp.float32).astype(jnp.bfloat16)
        partial_value = lax.optimization_barrier(partial_value)
        weight_acc = weight_acc + partial_value.astype(jnp.float32)
        back = jnp.dot(block_grad, value_weight.T, preferred_element_type=jnp.float32)
        input_grad = (block_res.astype(jnp.float32) + back).astype(jnp.bfloat16)
        table = table + jax.ops.segment_sum(input_grad.astype(jnp.float32), block_keys, NKEYS)
        return (weight_acc, table), None

    start = (jnp.zeros((D, HW), jnp.float32), jnp.zeros((NKEYS, D), jnp.float32))
    (weight_grad, key_grad), _ = lax.scan(step, start, (inputs, grads, residual, keys))
    return weight_grad, key_grad
```

```python
import jax
import jax.numpy as jnp
from jax import lax
from jax.sharding import PartitionSpec as P

F32, BF16 = jnp.float32, jnp.bfloat16
KEY_DEV = 256


def dot(a, b, ca, cb):
    return lax.dot_general(a, b, (((ca,), (cb,)), ((), ())), preferred_element_type=F32)


def general_body(layer_input, value_grad, residual_grad, value_weight, owner, key_row):
    all_heads = lax.all_gather(value_grad, "tp", axis=1, tiled=True)
    tok_rows, features = layer_input.shape
    groups = lax.axis_size("fsdp")
    slots = 2 * tok_rows // groups
    keys_here = KEY_DEV
    width = all_heads.shape[1]
    term = dot(layer_input, all_heads, 0, 0)
    pieces = term.astype(BF16).reshape(groups, features // groups, width)
    arrived = lax.all_to_all(pieces, "fsdp", split_axis=0, concat_axis=0, tiled=True)
    shard = jnp.sum(arrived.astype(F32), axis=0)
    back = dot(all_heads, lax.all_gather(value_weight, "fsdp", axis=0, tiled=True), 1, 1)
    input_grad = (residual_grad.astype(F32) + back).astype(BF16)
    target = owner[:, 0]
    onehot = (target[:, None] == jnp.arange(groups, dtype=jnp.int32)[None, :]).astype(jnp.int32)
    position = jnp.sum(jnp.cumsum(onehot, axis=0) * onehot, axis=1) - 1
    place = target * slots + position
    chooser = jnp.arange(groups * slots, dtype=jnp.int32)[:, None] == place[None, :]
    outgoing = dot(chooser.astype(BF16), input_grad, 1, 0).astype(BF16)
    out_keys = jnp.sum(jnp.where(chooser, key_row[None, :] + 1, 0), axis=1) - 1
    arrived = lax.all_to_all(outgoing, "fsdp", split_axis=0, concat_axis=0, tiled=True)
    arrived_keys = lax.all_to_all(out_keys, "fsdp", split_axis=0, concat_axis=0, tiled=True)
    selector = (arrived_keys[:, None] == jnp.arange(keys_here, dtype=jnp.int32)[None, :]).astype(BF16)
    table = dot(selector, arrived, 0, 0)
    return lax.psum(shard, "dp"), lax.psum(table, "dp")


def pair_body(layer_input, value_grad, residual_grad, value_weight, owner, key_row):
    core, z, t = (lax.axis_index(n) for n in ("dp", "fsdp", "tp"))
    tokens, features = layer_input.shape
    part = features // 4
    half = part // 2
    keys = KEY_DEV

    def core_swap(v):
        return lax.ppermute(v, "dp", [(0, 1), (1, 0)])

    def x_swap(v):
        return lax.ppermute(v, "tp", [(0, 1), (1, 0), (2, 3), (3, 2)])

    def y_swap(v):
        return lax.ppermute(v, "tp", [(0, 2), (2, 0), (1, 3), (3, 1)])

    def outer(v):
        return lax.ppermute(v, "fsdp", [(0, 1), (1, 0), (2, 3), (3, 2)])

    def inward(v):
        return lax.ppermute(v, "fsdp", [(0, 1), (3, 2)])

    def inner(v):
        return lax.ppermute(v, "fsdp", [(1, 2), (2, 1)])

    end = (z == 0) | (z == 3)
    beside = z ^ 1
    far_mid = jnp.where(z < 2, 2, 1)
    far_end = jnp.where(z < 2, 3, 0)

    def halves(v, which):
        return jnp.concatenate(
            [lax.dynamic_slice_in_dim(v, p * part + which * half, half, 1) for p in range(4)], 1
        )

    w_own = lax.dynamic_slice_in_dim(value_weight, core * half, half, 0)
    w_beside = outer(w_own)
    w_mid = inner(w_own)
    vx, vy = x_swap(value_grad), y_swap(value_grad)
    vd = jnp.concatenate([y_swap(vx[: tokens // 2]), x_swap(vy[tokens // 2 :])], 0)
    blocks = (value_grad, vx, vy, vd)
    heads = jnp.concatenate([lax.select_n(t ^ k, *blocks) for k in range(4)], 1)
    heads_other = core_swap(heads)
    in_other = core_swap(halves(layer_input, 1 - core))
    res_other = core_swap(halves(residual_grad, 1 - core))
    key = owner[:, 0] * keys + key_row
    key_other = core_swap(key)

    term = dot(halves(layer_input, core), heads, 0, 0) + dot(in_other, heads_other, 0, 0)
    term = term.reshape(4, half, -1)

    def piece(v, i):
        return lax.dynamic_index_in_dim(v, i, 0, keepdims=False)

    w_end = inner(w_beside)
    a1 = outer(jnp.where(end, piece(term, far_end).astype(BF16), w_mid))
    a2 = outer(jnp.where(end, piece(term, far_mid).astype(BF16), w_end))
    b2 = inner((piece(term, far_end) + a1.astype(F32)).astype(BF16))
    a3 = outer((piece(term, beside) + b2.astype(F32)).astype(BF16))
    b3 = inner((piece(term, far_mid) + a2.astype(F32)).astype(BF16))
    weight_half = piece(term, z) + a3.astype(F32) + b3.astype(F32)

    w_third = jnp.where(end, a1, w_mid)
    w_fourth = jnp.where(end, a2, w_end)
    arrived = (w_own, w_beside, w_third, w_fourth)
    order = [jnp.where(i == z, 0, jnp.where(i == beside, 1, jnp.where(i == far_mid, 2, 3))) for i in range(4)]
    weights = jnp.concatenate([lax.select_n(i, *arrived) for i in order], 0)

    def rows_grad(v, r):
        return (r.astype(F32) + dot(v, weights, 1, 1)).astype(BF16)

    def chooser(k):
        return (jnp.arange(4 * keys, dtype=jnp.int32)[:, None] == k[None, :]).astype(BF16)

    table = dot(chooser(key), rows_grad(heads, halves(residual_grad, core)), 1, 0)
    table = table + dot(chooser(key_other), rows_grad(heads_other, res_other), 1, 0)
    table = table.reshape(4, keys, -1)
    k1 = inward(piece(table, far_end).astype(BF16))
    k2 = inward(piece(table, far_mid).astype(BF16))
    l2 = inner((piece(table, far_end) + k1.astype(F32)).astype(BF16))
    k3 = outer((piece(table, beside) + l2.astype(F32)).astype(BF16))
    l3 = inner((piece(table, far_mid) + k2.astype(F32)).astype(BF16))
    key_half = piece(table, z) + k3.astype(F32) + l3.astype(F32)

    weight_pair = core_swap(weight_half)
    key_pair = core_swap(key_half)
    first = core == 0
    weight_grad = jnp.concatenate(
        [jnp.where(first, weight_half, weight_pair), jnp.where(first, weight_pair, weight_half)], 0
    )
    low, high = jnp.where(first, key_half, key_pair), jnp.where(first, key_pair, key_half)
    cols = []
    for p in range(4):
        cols += [low[:, p * half : (p + 1) * half], high[:, p * half : (p + 1) * half]]
    return weight_grad, jnp.concatenate(cols, 1)


def solution(mesh):
    shape = dict(mesh.shape)
    special = shape == {"dp": 2, "fsdp": 4, "tp": 4}
    return jax.shard_map(
        pair_body if special else general_body,
        mesh=mesh,
        in_specs=(
            P(("dp", "fsdp"), "tp"),
            P(("dp", "fsdp"), "tp"),
            P(("dp", "fsdp"), "tp"),
            P(("tp", "fsdp"), None),
            P(("dp", "fsdp"), None),
            P(("dp", "fsdp")),
        ),
        out_specs=(P(("tp", "fsdp"), None), P("fsdp", "tp")),
        check_vma=False,
    )
```

```python
import jax
import jax.numpy as jnp
from jax import lax
from jax.experimental import pallas as pl
from jax.experimental.pallas import tpu as pltpu
from jax.sharding import PartitionSpec as P

F32, BF16 = jnp.float32, jnp.bfloat16
KEY_DEV = 256


def dot(a, b, ca, cb):
    return lax.dot_general(a, b, (((ca,), (cb,)), ((), ())), preferred_element_type=F32)


def general_body(layer_input, value_grad, residual_grad, value_weight, owner, key_row):
    all_heads = lax.all_gather(value_grad, "tp", axis=1, tiled=True)
    tok_rows, features = layer_input.shape
    groups = lax.axis_size("fsdp")
    slots = 2 * tok_rows // groups
    keys_here = KEY_DEV
    width = all_heads.shape[1]
    term = dot(layer_input, all_heads, 0, 0)
    pieces = term.astype(BF16).reshape(groups, features // groups, width)
    arrived = lax.all_to_all(pieces, "fsdp", split_axis=0, concat_axis=0, tiled=True)
    shard = jnp.sum(arrived.astype(F32), axis=0)
    back = dot(all_heads, lax.all_gather(value_weight, "fsdp", axis=0, tiled=True), 1, 1)
    input_grad = (residual_grad.astype(F32) + back).astype(BF16)
    target = owner[:, 0]
    onehot = (target[:, None] == jnp.arange(groups, dtype=jnp.int32)[None, :]).astype(jnp.int32)
    position = jnp.sum(jnp.cumsum(onehot, axis=0) * onehot, axis=1) - 1
    place = target * slots + position
    chooser = jnp.arange(groups * slots, dtype=jnp.int32)[:, None] == place[None, :]
    outgoing = dot(chooser.astype(BF16), input_grad, 1, 0).astype(BF16)
    out_keys = jnp.sum(jnp.where(chooser, key_row[None, :] + 1, 0), axis=1) - 1
    arrived = lax.all_to_all(outgoing, "fsdp", split_axis=0, concat_axis=0, tiled=True)
    arrived_keys = lax.all_to_all(out_keys, "fsdp", split_axis=0, concat_axis=0, tiled=True)
    selector = (arrived_keys[:, None] == jnp.arange(keys_here, dtype=jnp.int32)[None, :]).astype(BF16)
    table = dot(selector, arrived, 0, 0)
    return lax.psum(shard, "dp"), lax.psum(table, "dp")


def term_kernel(*refs):
    mine, other, heads, out = refs[0], refs[1], refs[2:-1], refs[-1]
    rows, width = mine.shape[0], heads[0].shape[1]
    for i, head in enumerate(heads):
        out[:, i * width : (i + 1) * width] = dot(mine[...], head[:rows], 0, 0) + dot(other[...], head[rows:], 0, 0)


def back_kernel(shift, *refs):
    heads, (weight, residual, key, out, table) = refs[:8], refs[8:]
    step = pl.program_id(0)
    acc = residual[...].astype(F32)
    for i, head in enumerate(heads):
        k, side = i % 4, i // 4
        width = head.shape[1]
        start = pl.multiple_of(shift[k] + (shift[4] if side == 0 else width - shift[4]), width)
        acc = acc + dot(head[...], weight[:, pl.ds(start, width)], 1, 1)
    rows = acc.astype(BF16)
    index = lax.broadcasted_iota(jnp.int32, (table.shape[0], key.shape[2]), 0)
    add = dot(jnp.where(index == key[0], 1.0, 0.0).astype(BF16), rows, 1, 0)

    @pl.when(step == 0)
    def _():
        table[...] = add

    @pl.when(step > 0)
    def _():
        table[...] += add

    @pl.when(step == pl.num_programs(0) - 1)
    def _():
        out[...] = table[...].astype(BF16)


def join_kernel(shift, weight_mine, weight_pair, key_mine, key_pair, weight_out, key_out):
    core = shift[4]
    width = weight_mine.shape[1] // 4
    for k in range(4):
        cols = slice(k * width, (k + 1) * width)
        start = pl.multiple_of(shift[k] + core, width)
        weight_out[:, pl.ds(start, width)] = weight_mine[:, cols]
        start = pl.multiple_of(shift[k] + width - core, width)
        weight_out[:, pl.ds(start, width)] = weight_pair[:, cols]
    half = key_mine.shape[1] // 4
    first = core == 0
    for p in range(4):
        mine, pair = key_mine[:, p * half : (p + 1) * half], key_pair[:, p * half : (p + 1) * half]
        key_out[:, 2 * p * half : (2 * p + 1) * half] = jnp.where(first, mine, pair)
        key_out[:, (2 * p + 1) * half : (2 * p + 2) * half] = jnp.where(first, pair, mine)


def pair_body(layer_input, value_grad, residual_grad, value_weight, owner, key_row):
    core, z, t = (lax.axis_index(n) for n in ("dp", "fsdp", "tp"))
    tokens, features = layer_input.shape
    heads = value_grad.shape[1]
    part = features // 4
    half = part // 2
    wide = heads // 2
    keys = KEY_DEV
    phase = lax.optimization_barrier

    def core_swap(v):
        return lax.ppermute(v, "dp", [(0, 1), (1, 0)])

    def square(v, d):
        return lax.ppermute(v, "tp", [(i, i ^ d) for i in range(4)])

    def outer(v):
        return lax.ppermute(v, "fsdp", [(0, 1), (1, 0), (2, 3), (3, 2)])

    def inward(v):
        return lax.ppermute(v, "fsdp", [(0, 1), (3, 2)])

    def outward(v):
        return lax.ppermute(v, "fsdp", [(1, 0), (2, 3)])

    def inner(v):
        return lax.ppermute(v, "fsdp", [(1, 2), (2, 1)])

    end = (z == 0) | (z == 3)
    beside = z ^ 1
    far_mid = jnp.where(z < 2, 2, 1)
    far_end = jnp.where(z < 2, 3, 0)

    def halves(v, which):
        return jnp.concatenate(
            [lax.dynamic_slice_in_dim(v, p * part + which * half, half, 1) for p in range(4)], 1
        )

    w_own = lax.dynamic_slice_in_dim(value_weight, core * half, half, 0)
    w_beside, w_mid = outer(w_own), inner(w_own)
    v_other = core_swap(lax.dynamic_slice_in_dim(value_grad, (1 - core) * wide, wide, 1))
    v0 = jnp.concatenate([lax.dynamic_slice_in_dim(value_grad, core * wide, wide, 1), v_other], 0)
    key = owner[:, 0] * keys + key_row
    got = phase((w_beside, w_mid, square(v0, 1), square(v0, 2), core_swap(layer_input), core_swap(key),
                 core_swap(halves(residual_grad, 1 - core))))
    w_beside, w_mid, vx, vy, in_other, key_other, res_other = got

    vmem = pl.BlockSpec(memory_space=pltpu.VMEM)

    def term(*v):
        n = len(v)
        return pl.pallas_call(
            term_kernel,
            grid=(4,),
            out_shape=jax.ShapeDtypeStruct((features, n * wide), F32),
            in_specs=[pl.BlockSpec((tokens, part), lambda i: (0, i))] * 2
            + [pl.BlockSpec((2 * tokens, wide), lambda i: (0, 0))] * n,
            out_specs=pl.BlockSpec((part, n * wide), lambda i: (i, 0)),
            compiler_params=pltpu.CompilerParams(vmem_limit_bytes=32 << 20),
            cost_estimate=pl.CostEstimate(flops=n << 29, bytes_accessed=(2 + n * 2) << 20, transcendentals=0),
        )(layer_input, in_other, *v)

    first = term(v0, vx, vy)
    got = phase((outward(w_mid), inner(w_beside), square(vx[:tokens], 2), square(vy[tokens:], 1), first))
    w_third, w_end, vd0, vd1, first = got
    w_third = jnp.where(end, w_third, w_mid)

    vd = jnp.concatenate([vd0, vd1], 0)
    last = term(vd)

    def piece(i):
        return jnp.concatenate([lax.dynamic_slice_in_dim(v, i * part, part, 0) for v in (first, last)], 1)

    w_fourth = outward(w_end)
    i1 = inward(piece(far_end).astype(BF16))
    i2 = inward(piece(far_mid).astype(BF16))
    i3 = inward(piece(beside).astype(BF16))
    near = (v0, vx, vy, vd)
    far = core_swap(near)
    w_fourth, i1, far = phase((w_fourth, i1, far))
    w_fourth = jnp.where(end, w_fourth, w_end)
    b2 = inner((piece(far_end) + i1.astype(F32)).astype(BF16))
    b3 = inner((piece(far_mid) + i2.astype(F32)).astype(BF16))
    a3 = outward((piece(beside) + b2.astype(F32)).astype(BF16))
    weight_half = piece(z) + i3.astype(F32) + b3.astype(F32) + a3.astype(F32)
    weight_pair = core_swap(weight_half)

    arrived = (w_own, w_beside, w_third, w_fourth)
    order = [jnp.where(i == z, 0, jnp.where(i == beside, 1, jnp.where(i == far_mid, 2, 3))) for i in range(4)]
    weights = jnp.concatenate([lax.select_n(i, *arrived) for i in order], 0)
    shift = jnp.stack([(t ^ k) * heads for k in range(4)] + [core * wide]).astype(jnp.int32)
    residual = jnp.concatenate([halves(residual_grad, core), res_other], 0)
    rows = tokens // 2
    table = pl.pallas_call(
        back_kernel,
        grid=(4,),
        out_shape=jax.ShapeDtypeStruct((4 * keys, 4 * half), BF16),
        in_specs=[pl.BlockSpec(memory_space=pltpu.SMEM)]
        + [pl.BlockSpec((rows, wide), lambda i: (i, 0))] * 4
        + [pl.BlockSpec((rows, wide), lambda i: ((i + 2) % 4, 0))] * 4
        + [pl.BlockSpec((4 * half, 4 * heads), lambda i: (0, 0)),
           pl.BlockSpec((rows, 4 * half), lambda i: (i, 0)),
           pl.BlockSpec((1, 1, rows), lambda i: (i, 0, 0))],
        out_specs=pl.BlockSpec((4 * keys, 4 * half), lambda i: (0, 0)),
        scratch_shapes=[pltpu.VMEM((4 * keys, 4 * half), F32)],
        compiler_params=pltpu.CompilerParams(vmem_limit_bytes=40 << 20),
        cost_estimate=pl.CostEstimate(flops=3 << 30, bytes_accessed=8 << 20, transcendentals=0),
    )(shift, *near, *far, weights, residual, jnp.concatenate([key, key_other]).reshape(4, 1, rows))
    came = lax.all_to_all(table.reshape(4, keys, 4 * half), "fsdp", split_axis=0, concat_axis=0, tiled=True)
    key_half = jnp.sum(came.astype(F32), axis=0)
    key_pair = core_swap(key_half)

    return tuple(pl.pallas_call(
        join_kernel,
        out_shape=(jax.ShapeDtypeStruct((part, 4 * heads), F32), jax.ShapeDtypeStruct((keys, features), F32)),
        in_specs=[pl.BlockSpec(memory_space=pltpu.SMEM)] + [vmem] * 4,
        out_specs=(vmem, vmem),
        compiler_params=pltpu.CompilerParams(vmem_limit_bytes=16 << 20),
    )(shift, weight_half, weight_pair, key_half, key_pair))


def solution(mesh):
    shape = dict(mesh.shape)
    special = shape == {"dp": 2, "fsdp": 4, "tp": 4}
    return jax.shard_map(
        pair_body if special else general_body,
        mesh=mesh,
        in_specs=(
            P(("dp", "fsdp"), "tp"),
            P(("dp", "fsdp"), "tp"),
            P(("dp", "fsdp"), "tp"),
            P(("tp", "fsdp"), None),
            P(("dp", "fsdp"), None),
            P(("dp", "fsdp")),
        ),
        out_specs=(P(("tp", "fsdp"), None), P("fsdp", "tp")),
        check_vma=False,
    )
```

```python
import jax
import jax.numpy as jnp
from jax import lax
from jax.experimental import pallas as pl
from jax.experimental.pallas import tpu as pltpu
from jax.sharding import PartitionSpec as P

F32, BF16 = jnp.float32, jnp.bfloat16
KEY_DEV = 256


def dot(a, b, ca, cb):
    return lax.dot_general(a, b, (((ca,), (cb,)), ((), ())), preferred_element_type=F32)


def general_body(layer_input, value_grad, residual_grad, value_weight, owner, key_row):
    all_heads = lax.all_gather(value_grad, "tp", axis=1, tiled=True)
    tok_rows, features = layer_input.shape
    groups = lax.axis_size("fsdp")
    slots = 2 * tok_rows // groups
    keys_here = KEY_DEV
    width = all_heads.shape[1]
    term = dot(layer_input, all_heads, 0, 0)
    pieces = term.astype(BF16).reshape(groups, features // groups, width)
    arrived = lax.all_to_all(pieces, "fsdp", split_axis=0, concat_axis=0, tiled=True)
    shard = jnp.sum(arrived.astype(F32), axis=0)
    back = dot(all_heads, lax.all_gather(value_weight, "fsdp", axis=0, tiled=True), 1, 1)
    input_grad = (residual_grad.astype(F32) + back).astype(BF16)
    target = owner[:, 0]
    onehot = (target[:, None] == jnp.arange(groups, dtype=jnp.int32)[None, :]).astype(jnp.int32)
    position = jnp.sum(jnp.cumsum(onehot, axis=0) * onehot, axis=1) - 1
    place = target * slots + position
    chooser = jnp.arange(groups * slots, dtype=jnp.int32)[:, None] == place[None, :]
    outgoing = dot(chooser.astype(BF16), input_grad, 1, 0).astype(BF16)
    out_keys = jnp.sum(jnp.where(chooser, key_row[None, :] + 1, 0), axis=1) - 1
    arrived = lax.all_to_all(outgoing, "fsdp", split_axis=0, concat_axis=0, tiled=True)
    arrived_keys = lax.all_to_all(out_keys, "fsdp", split_axis=0, concat_axis=0, tiled=True)
    selector = (arrived_keys[:, None] == jnp.arange(keys_here, dtype=jnp.int32)[None, :]).astype(BF16)
    table = dot(selector, arrived, 0, 0)
    return lax.psum(shard, "dp"), lax.psum(table, "dp")


def term_kernel(place, *refs):
    n = sum(r.shape == refs[8].shape for r in refs[8:]) // 2
    inputs, heads, out, sends = refs[:8], refs[8 : 8 + 2 * n], refs[8 + 2 * n], refs[9 + 2 * n :]
    width = heads[0].shape[1]
    for side in range(2):
        turned = jnp.concatenate([r[...] for r in inputs[4 * side : 4 * side + 4]], 1).T
        for k in range(n):
            add = dot(turned, heads[n * side + k][...], 1, 0)
            cols = slice(k * width, (k + 1) * width)
            if side == 0:
                out[:, cols] = add
            else:
                out[:, cols] += add
    row = 0
    for send in sends:
        send[...] = out[row : row + send.shape[0], :].astype(BF16)
        row += send.shape[0]


def back_kernel(place, *refs):
    residuals, heads, refs = refs[:8], refs[8:16], refs[16:]
    own, beside, mid, end, third, fourth, key, send, keep, weight = refs
    half, width = own.shape[0], heads[0].shape[1]
    tokens = heads[0].shape[0]
    keys = keep.shape[0] // 2

    def put(which, ref):
        weight[pl.ds(pl.multiple_of(place[which] * half, half), half), :] = ref[...]

    put(5, own)
    put(6, beside)

    @pl.when(place[9] == 1)
    def _():
        put(7, third)
        put(8, fourth)

    @pl.when(place[9] == 0)
    def _():
        put(7, mid)
        put(8, end)

    row = lax.broadcasted_iota(jnp.int32, (keys, tokens), 0)
    total = [None] * 2
    for side in range(2):
        acc = jnp.concatenate([r[...] for r in residuals[4 * side : 4 * side + 4]], 1).astype(F32)
        for k in range(4):
            cols = pl.ds(pl.multiple_of(place[k] * width, width), width)
            acc = acc + dot(heads[4 * side + k][...], weight[:, cols], 1, 1)
        rows = acc.astype(BF16)
        for i in range(2):
            chosen = jnp.concatenate(
                [(row + place[10 + 2 * i + j] * keys) == key[side : side + 1, :] for j in range(2)], 0
            )
            add = dot(jnp.where(chosen, 1.0, 0.0).astype(BF16), rows, 1, 0)
            total[i] = add if side == 0 else total[i] + add
    send[...] = total[0].astype(BF16)
    keep[...] = total[1]


def join_weight_kernel(place, mine, pair, out):
    half, width = mine.shape[0], mine.shape[1] // 4
    here = pl.multiple_of(place[4] * half, half)
    there = pl.multiple_of(half - place[4] * half, half)
    for k in range(4):
        start = pl.multiple_of(place[k] * width, width)
        out[pl.ds(here, half), pl.ds(start, width)] = mine[:, k * width : (k + 1) * width]
        out[pl.ds(there, half), pl.ds(start, width)] = pair[:, k * width : (k + 1) * width]


def join_key_kernel(place, mine, pair, out):
    first = place[4] == 0
    half = mine.shape[1] // 4
    for p in range(4):
        a, b = mine[:, p * half : (p + 1) * half], pair[:, p * half : (p + 1) * half]
        out[:, 2 * p * half : (2 * p + 1) * half] = jnp.where(first, a, b)
        out[:, (2 * p + 1) * half : (2 * p + 2) * half] = jnp.where(first, b, a)


def pair_body(layer_input, value_grad, residual_grad, value_weight, owner, key_row):
    core, z, t = (lax.axis_index(n) for n in ("dp", "fsdp", "tp"))
    tokens, features = layer_input.shape
    heads = value_grad.shape[1]
    part = features // 4
    half = part // 2
    keys = KEY_DEV
    phase = lax.optimization_barrier

    def core_swap(v):
        return lax.ppermute(v, "dp", [(0, 1), (1, 0)])

    def outer(v):
        return lax.ppermute(v, "fsdp", [(0, 1), (1, 0), (2, 3), (3, 2)])

    def inward(v):
        return lax.ppermute(v, "fsdp", [(0, 1), (3, 2)])

    def outward(v):
        return lax.ppermute(v, "fsdp", [(1, 0), (2, 3)])

    def inner(v):
        return lax.ppermute(v, "fsdp", [(1, 2), (2, 1)])

    end = ((z == 0) | (z == 3)).astype(jnp.int32)
    low = z < 2
    beside = z ^ 1
    far_mid = jnp.where(low, 2, 1)
    far_end = jnp.where(low, 3, 0)
    place = jnp.stack([t, t ^ 1, t ^ 2, t ^ 3, core, z, beside, far_mid, far_end, end, z ^ 1, z ^ 3, z, z ^ 2]).astype(jnp.int32)
    ranked = [pl.BlockSpec((tokens, half), lambda i, s, r=r: (0, 2 * s[r] + s[4])) for r in (8, 7, 6, 5)]
    split = [pl.BlockSpec((tokens, half), lambda i, s, p=p: (0, 2 * p + s[4])) for p in range(4)]

    def whole(*shape):
        return pl.BlockSpec(shape, lambda i, s: (0,) * len(shape))

    def call(kernel, out, in_specs, scratch, flops, *args):
        return pl.pallas_call(
            kernel,
            out_shape=out,
            grid_spec=pltpu.PrefetchScalarGridSpec(
                num_scalar_prefetch=1, grid=(1,), in_specs=in_specs,
                out_specs=jax.tree.map(lambda o: whole(*o.shape), out), scratch_shapes=scratch,
            ),
            compiler_params=pltpu.CompilerParams(vmem_limit_bytes=40 << 20),
            cost_estimate=pl.CostEstimate(flops=flops, bytes_accessed=6 << 20, transcendentals=0),
        )(place, *args)

    def square(v, d):
        return lax.ppermute(v, "tp", [(i, i ^ d) for i in range(4)])

    def across(v):
        return lax.ppermute(v, "fsdp", [(i, i ^ 2) for i in range(4)])

    def struct(rows, cols, dtype):
        return jax.ShapeDtypeStruct((rows, cols), dtype)

    def term(v, sends):
        n = len(v) // 2
        out = (struct(4 * half, n * heads, F32),) + tuple(struct(r, n * heads, BF16) for r in sends)
        return call(
            term_kernel, out, ranked * 2 + [whole(tokens, heads)] * (2 * n), [], n << 29,
            *([layer_input] * 4), *([in_other] * 4), *v,
        )

    def plus(v, came):
        return (v + came.astype(F32)).astype(BF16)

    v0 = value_grad
    v0_other, weight_rows = phase((core_swap(v0), value_weight))
    in_other = core_swap(layer_input)
    w_own = lax.dynamic_slice_in_dim(weight_rows, core * half, half, 0)
    got = phase((outer(w_own), inner(w_own), square(v0, 1), square(v0, 2), in_other))
    w_beside, w_mid, vx, vy, in_other = got

    vx_other, vy_other = core_swap(vx), core_swap(vy)
    term1, send1, send2 = term((v0, vx, vy, v0_other, vx_other, vy_other), (half, half))
    i1, i2 = inward(send1), inward(send2)
    key = owner[:, 0] * keys + key_row
    w_third, w_end, vd, term1 = phase((outward(w_mid), inner(w_beside), square(v0, 3), term1))

    vd_other = core_swap(vd)
    term2, send3 = term((vd, vd_other), (2 * half,))
    res_other, key_other = core_swap(residual_grad), core_swap(key)
    i1, w_fourth, term2, res_other, key_other = phase((i1, outward(w_end), term2, res_other, key_other))

    b1 = inner(plus(term1[:half], i1))
    i3 = inward(send3)
    send, keep = call(
        back_kernel, (struct(2 * keys, 4 * half, BF16), struct(2 * keys, 4 * half, F32)),
        split * 2 + [whole(tokens, heads)] * 8 + [whole(half, 4 * heads)] * 6 + [whole(2, tokens)],
        [pltpu.VMEM((4 * half, 4 * heads), BF16)], 3 << 30,
        *([residual_grad] * 4), *([res_other] * 4), v0, vx, vy, vd, v0_other, vx_other, vy_other, vd_other,
        w_own, w_beside, w_mid, w_end, w_third, w_fourth, jnp.stack([key, key_other]),
    )
    send, keep, b1, i2 = phase((send, keep, b1, i2))

    k1 = outer(send)
    b2 = inner(plus(term1[half : 2 * half], i2))
    a1 = outward(plus(term1[2 * half : 3 * half], b1))
    i4 = inward(jnp.concatenate([v[2 * half : 3 * half].astype(BF16) for v in (term1, term2)], 1))
    b3 = inner(plus(term2[: 2 * half], i3))
    k1, b2, i3 = phase((k1, b2, i3))
    k2 = across(plus(keep[keys:], k1[keys:]))
    a3 = outward(plus(term2[2 * half : 3 * half], b3[:half]))
    key_half = keep[:keys] + k1[:keys].astype(F32) + k2.astype(F32)

    def total(v, *came):
        return sum((c.astype(F32) for c in came), v[3 * half :])

    weight_half = jnp.concatenate([
        total(term1, i4[:, : 3 * heads], b2, a1), total(term2, i4[:, 3 * heads :], b3[half:], a3),
    ], 1)
    weight_pair = core_swap(weight_half)
    key_pair = core_swap(key_half)

    weight_grad = call(
        join_weight_kernel, jax.ShapeDtypeStruct((part, 4 * heads), F32),
        [whole(half, 4 * heads)] * 2, [], 0, weight_half, weight_pair,
    )
    key_grad = call(
        join_key_kernel, jax.ShapeDtypeStruct((keys, features), F32),
        [whole(keys, 4 * half)] * 2, [], 0, key_half, key_pair,
    )
    return weight_grad, key_grad


def solution(mesh):
    shape = dict(mesh.shape)
    special = shape == {"dp": 2, "fsdp": 4, "tp": 4}
    return jax.shard_map(
        pair_body if special else general_body,
        mesh=mesh,
        in_specs=(
            P(("dp", "fsdp"), "tp"),
            P(("dp", "fsdp"), "tp"),
            P(("dp", "fsdp"), "tp"),
            P(("tp", "fsdp"), None),
            P(("dp", "fsdp"), None),
            P(("dp", "fsdp")),
        ),
        out_specs=(P(("tp", "fsdp"), None), P("fsdp", "tp")),
        check_vma=False,
    )
```

```python
import functools

import jax
import jax.numpy as jnp
from jax import lax
from jax.experimental import pallas as pl
from jax.experimental.pallas import tpu as pltpu
from jax.sharding import PartitionSpec as P

F32, BF16 = jnp.float32, jnp.bfloat16
KEY_DEV = 256


def dot(a, b, ca, cb):
    return lax.dot_general(a, b, (((ca,), (cb,)), ((), ())), preferred_element_type=F32)


def general_body(layer_input, value_grad, residual_grad, value_weight, owner, key_row):
    all_heads = lax.all_gather(value_grad, "tp", axis=1, tiled=True)
    tok_rows, features = layer_input.shape
    groups = lax.axis_size("fsdp")
    slots = 2 * tok_rows // groups
    keys_here = KEY_DEV
    width = all_heads.shape[1]
    term = dot(layer_input, all_heads, 0, 0)
    pieces = term.astype(BF16).reshape(groups, features // groups, width)
    arrived = lax.all_to_all(pieces, "fsdp", split_axis=0, concat_axis=0, tiled=True)
    shard = jnp.sum(arrived.astype(F32), axis=0)
    back = dot(all_heads, lax.all_gather(value_weight, "fsdp", axis=0, tiled=True), 1, 1)
    input_grad = (residual_grad.astype(F32) + back).astype(BF16)
    target = owner[:, 0]
    onehot = (target[:, None] == jnp.arange(groups, dtype=jnp.int32)[None, :]).astype(jnp.int32)
    position = jnp.sum(jnp.cumsum(onehot, axis=0) * onehot, axis=1) - 1
    place = target * slots + position
    chooser = jnp.arange(groups * slots, dtype=jnp.int32)[:, None] == place[None, :]
    outgoing = dot(chooser.astype(BF16), input_grad, 1, 0).astype(BF16)
    out_keys = jnp.sum(jnp.where(chooser, key_row[None, :] + 1, 0), axis=1) - 1
    arrived = lax.all_to_all(outgoing, "fsdp", split_axis=0, concat_axis=0, tiled=True)
    arrived_keys = lax.all_to_all(out_keys, "fsdp", split_axis=0, concat_axis=0, tiled=True)
    selector = (arrived_keys[:, None] == jnp.arange(keys_here, dtype=jnp.int32)[None, :]).astype(BF16)
    table = dot(selector, arrived, 0, 0)
    return lax.psum(shard, "dp"), lax.psum(table, "dp")


def turn_kernel(place, mine, other, out):
    half = mine.shape[1] // 8
    for side, ref in enumerate((mine, other)):
        for i, rank in enumerate((8, 7, 6, 5)):
            cols = pl.ds(pl.multiple_of((2 * place[rank] + place[4]) * half, half), half)
            out[side, i * half : (i + 1) * half, :] = ref[:, cols].T


def term_kernel(rounded, place, turned, *refs):
    n = sum(r.shape == refs[0].shape for r in refs) // 2
    heads, out, sends = refs[: 2 * n], refs[2 * n], refs[1 + 2 * n :]
    width = heads[0].shape[1]
    for k in range(n):
        cols = slice(k * width, (k + 1) * width)
        out[:, cols] = dot(turned[0], heads[k][...], 1, 0) + dot(turned[1], heads[n + k][...], 1, 0)
    half, wide = out.shape[0] // 4, out.shape[1]
    for first, send in zip(rounded, sends):
        for j in range(send.shape[1] // wide):
            row = (first + j) * half
            send[:, j * wide : (j + 1) * wide] = out[row : row + half, :].astype(BF16)


def choose_kernel(place, key, out):
    keys = out.shape[0] // 4
    row = lax.broadcasted_iota(jnp.int32, (keys, key.shape[1]), 0)
    for j in range(4):
        hit = row + place[10 + j] * keys == key[...]
        out[j * keys : (j + 1) * keys, :] = jnp.where(hit, 1.0, 0.0).astype(BF16)


def back_kernel(base, ranks, place, *refs):
    residuals, heads, chosen, weights, (send, keep, weight) = refs[:2], refs[2:10], refs[10], refs[11:-3], refs[-3:]
    half, width = weights[0].shape[0], heads[0].shape[1]
    tokens = heads[0].shape[0]
    first = place[base]

    def put(rank, ref):
        weight[pl.ds(pl.multiple_of((place[rank] - first) * half, half), half), :] = ref[...]

    for rank, ref in zip(ranks[:-1], weights):
        put(rank, ref)
    for here in range(2):
        pl.when(place[9] == here)(lambda here=here: put(ranks[-1], weights[len(ranks) - 1 + here]))

    total = [None] * 2
    starts = [pl.multiple_of((2 * (first + p) + place[4]) * half, half) for p in range(len(ranks))]
    for side in range(2):
        acc = jnp.concatenate([residuals[side][:, pl.ds(at, half)] for at in starts], 1).astype(F32)
        for k in range(4):
            cols = pl.ds(pl.multiple_of(place[k] * width, width), width)
            acc = acc + dot(heads[4 * side + k][...], weight[:, cols], 1, 1)
        rows = acc.astype(BF16)
        for i in range(2):
            size = send.shape[0]
            pick = chosen[i * size : (i + 1) * size, side * tokens : (side + 1) * tokens]
            add = dot(pick, rows, 1, 0)
            total[i] = add if side == 0 else total[i] + add
    send[...] = total[0].astype(BF16)
    keep[...] = total[1]


def join_weight_kernel(place, mine, pair, out):
    half, width = mine.shape[0], mine.shape[1] // 4
    here = pl.multiple_of(place[4] * half, half)
    there = pl.multiple_of(half - place[4] * half, half)
    for k in range(4):
        start = pl.multiple_of(place[k] * width, width)
        out[pl.ds(here, half), pl.ds(start, width)] = mine[:, k * width : (k + 1) * width]
        out[pl.ds(there, half), pl.ds(start, width)] = pair[:, k * width : (k + 1) * width]


def join_key_kernel(place, mine, pair, out):
    first = place[4] == 0
    half = mine.shape[1] // 4
    for p in range(4):
        a, b = mine[:, p * half : (p + 1) * half], pair[:, p * half : (p + 1) * half]
        out[:, 2 * p * half : (2 * p + 1) * half] = jnp.where(first, a, b)
        out[:, (2 * p + 1) * half : (2 * p + 2) * half] = jnp.where(first, b, a)


def pair_body(layer_input, value_grad, residual_grad, value_weight, owner, key_row):
    core, z, t = (lax.axis_index(n) for n in ("dp", "fsdp", "tp"))
    tokens, features = layer_input.shape
    heads = value_grad.shape[1]
    part = features // 4
    half = part // 2
    keys = KEY_DEV
    phase = lax.optimization_barrier

    def core_swap(v):
        return lax.ppermute(v, "dp", [(0, 1), (1, 0)])

    def outer(v):
        return lax.ppermute(v, "fsdp", [(0, 1), (1, 0), (2, 3), (3, 2)])

    def inward(v):
        return lax.ppermute(v, "fsdp", [(0, 1), (3, 2)])

    def outward(v):
        return lax.ppermute(v, "fsdp", [(1, 0), (2, 3)])

    def inner(v):
        return lax.ppermute(v, "fsdp", [(1, 2), (2, 1)])

    end = ((z == 0) | (z == 3)).astype(jnp.int32)
    low = (z < 2).astype(jnp.int32)
    beside = z ^ 1
    far_mid = 1 + low
    far_end = 3 * low
    place = jnp.stack([t, t ^ 1, t ^ 2, t ^ 3, core, z, beside, far_mid, far_end, end, z ^ 1, z ^ 3, z, z ^ 2, 1 - low]).astype(jnp.int32)
    smem, vmem = pl.BlockSpec(memory_space=pltpu.SMEM), pl.BlockSpec(memory_space=pltpu.VMEM)

    def call(kernel, out, scratch, flops, *args):
        return pl.pallas_call(
            kernel,
            out_shape=out,
            in_specs=[smem] + [vmem] * len(args),
            out_specs=jax.tree.map(lambda o: vmem, out),
            scratch_shapes=scratch,
            compiler_params=pltpu.CompilerParams(vmem_limit_bytes=16 << 20),
            cost_estimate=pl.CostEstimate(flops=flops, bytes_accessed=1 << 20, transcendentals=0),
        )(place, *args)

    def square(v, d):
        return lax.ppermute(v, "tp", [(i, i ^ d) for i in range(4)])

    def across(v):
        return lax.ppermute(v, "fsdp", [(i, i ^ 2) for i in range(4)])

    def struct(rows, cols, dtype):
        return jax.ShapeDtypeStruct((rows, cols), dtype)

    def term(v, *parts):
        n = len(v) // 2 * heads
        out = (struct(4 * half, n, F32),) + tuple(struct(half, count * n, BF16) for _, count in parts)
        kernel = functools.partial(term_kernel, tuple(first for first, _ in parts))
        return call(kernel, out, [], n << 20, turned, *v)

    def plus(v, came):
        return (v + came.astype(F32)).astype(BF16)

    def far_plus(v, came):
        n = v.shape[1]
        return jnp.concatenate([plus(v[:half], came[:, :n]), plus(v[half : 2 * half], came[:, n : 2 * n])], 1)

    def back(base, ranks, *weights):
        n = len(ranks) * half
        return call(
            functools.partial(back_kernel, base, ranks),
            (struct(2 * keys, n, BF16), struct(2 * keys, n, F32)),
            [pltpu.VMEM((n, 4 * heads), BF16)], len(ranks) * (3 << 28),
            residual_grad, res_other, v0, vx, vy, vd, v0_other, vx_other, vy_other, vd_other, chosen, *weights,
        )

    v0 = value_grad
    v0_other, weight_rows = phase((core_swap(v0), value_weight))
    w_own = lax.dynamic_slice_in_dim(weight_rows, core * half, half, 0)
    in_other, res_other = core_swap(layer_input), core_swap(residual_grad)
    turned = call(turn_kernel, jax.ShapeDtypeStruct((2, 4 * half, tokens), BF16), [], 0, layer_input, in_other)
    term0, send0 = term((v0, v0_other), (0, 4))
    got = phase((outer(w_own), inner(w_own), square(v0, 1), square(v0, 2), turned, term0, send0,
                 res_other, low == 1, end == 1))
    w_beside, w_mid, vx, vy, turned, term0, send0, res_other, is_low, is_end = got

    vx_other, vy_other = core_swap(vx), core_swap(vy)
    term1, send1, near1 = term((vx, vy, vx_other, vy_other), (0, 2), (2, 1))
    key = owner[:, 0] * keys + key_row
    got = phase((outer(jnp.where(is_end, send0, w_mid)), inner(w_beside), square(v0, 3), term1, send1, near1,
                 core_swap(key)))
    i0, w_end, vd, term1, send1, near1, key_other = got
    w_third = i0

    b0 = inner(far_plus(term0, i0))
    vd_other = core_swap(vd)
    key_both = jnp.concatenate([key, key_other])[None, :]
    chosen = call(choose_kernel, struct(4 * keys, 2 * tokens, BF16), [], 0, key_both)
    term2, send2, near2 = term((vd, vd_other), (0, 2), (2, 1))
    i2 = inward(send2)
    send_a, keep_a = back(14, (5, 6, 7), w_own, w_beside, w_mid, w_third)
    got = phase((outer(jnp.where(is_end, send1, w_end)), b0, term1, term2, send_a, keep_a, term0, near1, near2))
    i1, b0, term1, term2, send_a, keep_a, term0, near1, near2 = got
    w_fourth = i1

    def joined(a, b):
        return jnp.where(is_low, jnp.concatenate([a, b], 1), jnp.concatenate([b, a], 1))

    send_b, keep_b = back(8, (8,), w_end, w_fourth)
    keep = joined(keep_a, keep_b)
    b1 = inner(far_plus(term1, i1))
    b2 = inner(far_plus(term2, i2))
    k1, b1, b2, term1, term2, keep = phase((outer(joined(send_a, send_b)), b1, b2, term1, term2, keep))

    k2 = across(plus(keep[keys:], k1[keys:]))
    mine = keep[:keys] + k1[:keys].astype(F32)
    back1 = plus(term1[2 * half : 3 * half], b1[:, : 2 * heads])
    back0 = plus(term0[2 * half : 3 * half], b0[:, :heads])
    back2 = plus(term2[2 * half : 3 * half], b2[:, :heads])
    i3 = outer(jnp.where(
        is_end, jnp.concatenate([near1, near2, near2], 1), jnp.concatenate([back1, back2, back0], 1)
    ))

    def total(v, *came):
        return sum((c.astype(F32) for c in came), v[3 * half :])

    weight_half = jnp.concatenate([
        total(term0, jnp.where(is_end, i3[:, 3 * heads :], i0[:, 2 * heads : 3 * heads]), b0[:, heads:]),
        total(term1, i3[:, : 2 * heads], b1[:, 2 * heads :]),
        total(term2, i3[:, 2 * heads : 3 * heads], b2[:, heads:]),
    ], 1)
    weight_pair = core_swap(weight_half)
    weight_grad = call(
        join_weight_kernel, jax.ShapeDtypeStruct((part, 4 * heads), F32),
        [], 0, weight_half, weight_pair,
    )
    key_half = mine + k2.astype(F32)
    key_pair = core_swap(key_half)
    key_grad = call(
        join_key_kernel, jax.ShapeDtypeStruct((keys, features), F32),
        [], 0, key_half, key_pair,
    )
    return weight_grad, key_grad


def solution(mesh):
    shape = dict(mesh.shape)
    special = shape == {"dp": 2, "fsdp": 4, "tp": 4}
    return jax.shard_map(
        pair_body if special else general_body,
        mesh=mesh,
        in_specs=(
            P(("dp", "fsdp"), "tp"),
            P(("dp", "fsdp"), "tp"),
            P(("dp", "fsdp"), "tp"),
            P(("tp", "fsdp"), None),
            P(("dp", "fsdp"), None),
            P(("dp", "fsdp")),
        ),
        out_specs=(P(("tp", "fsdp"), None), P("fsdp", "tp")),
        check_vma=False,
    )
```

```python
import functools

import jax
import jax.numpy as jnp
from jax import lax
from jax.experimental import pallas as pl
from jax.experimental.pallas import tpu as pltpu
from jax.sharding import PartitionSpec as P

F32, BF16 = jnp.float32, jnp.bfloat16
KEY_DEV = 256


def dot(a, b, ca, cb):
    return lax.dot_general(a, b, (((ca,), (cb,)), ((), ())), preferred_element_type=F32)


def general_body(layer_input, value_grad, residual_grad, value_weight, owner, key_row):
    all_heads = lax.all_gather(value_grad, "tp", axis=1, tiled=True)
    tok_rows, features = layer_input.shape
    groups = lax.axis_size("fsdp")
    slots = 2 * tok_rows // groups
    keys_here = KEY_DEV
    width = all_heads.shape[1]
    term = dot(layer_input, all_heads, 0, 0)
    pieces = term.astype(BF16).reshape(groups, features // groups, width)
    arrived = lax.all_to_all(pieces, "fsdp", split_axis=0, concat_axis=0, tiled=True)
    shard = jnp.sum(arrived.astype(F32), axis=0)
    back = dot(all_heads, lax.all_gather(value_weight, "fsdp", axis=0, tiled=True), 1, 1)
    input_grad = (residual_grad.astype(F32) + back).astype(BF16)
    target = owner[:, 0]
    onehot = (target[:, None] == jnp.arange(groups, dtype=jnp.int32)[None, :]).astype(jnp.int32)
    position = jnp.sum(jnp.cumsum(onehot, axis=0) * onehot, axis=1) - 1
    place = target * slots + position
    chooser = jnp.arange(groups * slots, dtype=jnp.int32)[:, None] == place[None, :]
    outgoing = dot(chooser.astype(BF16), input_grad, 1, 0).astype(BF16)
    out_keys = jnp.sum(jnp.where(chooser, key_row[None, :] + 1, 0), axis=1) - 1
    arrived = lax.all_to_all(outgoing, "fsdp", split_axis=0, concat_axis=0, tiled=True)
    arrived_keys = lax.all_to_all(out_keys, "fsdp", split_axis=0, concat_axis=0, tiled=True)
    selector = (arrived_keys[:, None] == jnp.arange(keys_here, dtype=jnp.int32)[None, :]).astype(BF16)
    table = dot(selector, arrived, 0, 0)
    return lax.psum(shard, "dp"), lax.psum(table, "dp")


def turn_kernel(place, mine, other, out):
    half = mine.shape[1] // 8
    for side, ref in enumerate((mine, other)):
        for i, rank in enumerate((8, 7, 6, 5)):
            cols = pl.ds(pl.multiple_of((2 * place[rank] + place[4]) * half, half), half)
            out[side, i * half : (i + 1) * half, :] = ref[:, cols].T


def term_kernel(rounded, place, turned, *refs):
    n = sum(r.shape == refs[0].shape for r in refs) // 2
    heads, out, sends = refs[: 2 * n], refs[2 * n], refs[1 + 2 * n :]
    width = heads[0].shape[1]
    for k in range(n):
        cols = slice(k * width, (k + 1) * width)
        out[:, cols] = dot(turned[0], heads[k][...], 1, 0) + dot(turned[1], heads[n + k][...], 1, 0)
    half, wide = out.shape[0] // 4, out.shape[1]
    for first, send in zip(rounded, sends):
        for j in range(send.shape[1] // wide):
            row = (first + j) * half
            send[:, j * wide : (j + 1) * wide] = out[row : row + half, :].astype(BF16)


def choose_kernel(place, key, out):
    keys = out.shape[0] // 4
    row = lax.broadcasted_iota(jnp.int32, (keys, key.shape[1]), 0)
    for j in range(4):
        hit = row + place[10 + j] * keys == key[...]
        out[j * keys : (j + 1) * keys, :] = jnp.where(hit, 1.0, 0.0).astype(BF16)


def back_kernel(base, ranks, place, *refs):
    residuals, heads, chosen, weights, (send, keep, weight) = refs[:2], refs[2:10], refs[10], refs[11:-3], refs[-3:]
    half, width = weights[0].shape[0], heads[0].shape[1]
    tokens = heads[0].shape[0]
    first = place[base]

    def put(rank, ref):
        weight[pl.ds(pl.multiple_of((place[rank] - first) * half, half), half), :] = ref[...]

    for rank, ref in zip(ranks[:-1], weights):
        put(rank, ref)
    for here in range(2):
        pl.when(place[9] == here)(lambda here=here: put(ranks[-1], weights[len(ranks) - 1 + here]))

    total = [None] * 2
    starts = [pl.multiple_of((2 * (first + p) + place[4]) * half, half) for p in range(len(ranks))]
    for side in range(2):
        acc = jnp.concatenate([residuals[side][:, pl.ds(at, half)] for at in starts], 1).astype(F32)
        for k in range(4):
            cols = pl.ds(pl.multiple_of(place[k] * width, width), width)
            acc = acc + dot(heads[4 * side + k][...], weight[:, cols], 1, 1)
        rows = acc.astype(BF16)
        for i in range(2):
            size = send.shape[0]
            pick = chosen[i * size : (i + 1) * size, side * tokens : (side + 1) * tokens]
            add = dot(pick, rows, 1, 0)
            total[i] = add if side == 0 else total[i] + add
    send[...] = total[0].astype(BF16)
    keep[...] = total[1]


def join_weight_kernel(place, mine, pair, last, last_pair, out, done):
    half, width = mine.shape[0], mine.shape[1] // 4
    here = pl.multiple_of(place[4] * half, half)
    there = pl.multiple_of(half - place[4] * half, half)
    for at, kept, came in ((here, mine, last), (there, pair, last_pair)):
        for k in range(4):
            start = pl.multiple_of(place[k] * width, width)
            value = kept[:, k * width : (k + 1) * width]
            if k > 0:
                value = value + came[:, (k - 1) * width : k * width].astype(F32)
            out[pl.ds(at, half), pl.ds(start, width)] = value
    done[...] = jnp.zeros_like(done)


def join_key_kernel(place, before, mine, pair, last, last_pair, out):
    first = place[4] == 0
    half = mine.shape[1] // 4
    for p in range(4):
        cols = slice(p * half, (p + 1) * half)
        a = mine[:, cols] + last[:, cols].astype(F32)
        b = pair[:, cols] + last_pair[:, cols].astype(F32)
        out[:, 2 * p * half : (2 * p + 1) * half] = jnp.where(first, a, b)
        out[:, (2 * p + 1) * half : (2 * p + 2) * half] = jnp.where(first, b, a)


def pair_body(layer_input, value_grad, residual_grad, value_weight, owner, key_row):
    core, z, t = (lax.axis_index(n) for n in ("dp", "fsdp", "tp"))
    tokens, features = layer_input.shape
    heads = value_grad.shape[1]
    part = features // 4
    half = part // 2
    keys = KEY_DEV
    phase = lax.optimization_barrier

    def core_swap(v):
        return lax.ppermute(v, "dp", [(0, 1), (1, 0)])

    def outer(v):
        return lax.ppermute(v, "fsdp", [(0, 1), (1, 0), (2, 3), (3, 2)])

    def inward(v):
        return lax.ppermute(v, "fsdp", [(0, 1), (3, 2)])

    def outward(v):
        return lax.ppermute(v, "fsdp", [(1, 0), (2, 3)])

    def inner(v):
        return lax.ppermute(v, "fsdp", [(1, 2), (2, 1)])

    end = ((z == 0) | (z == 3)).astype(jnp.int32)
    low = (z < 2).astype(jnp.int32)
    beside = z ^ 1
    far_mid = 1 + low
    far_end = 3 * low
    place = jnp.stack([t, t ^ 1, t ^ 2, t ^ 3, core, z, beside, far_mid, far_end, end, z ^ 1, z ^ 3, z, z ^ 2, 1 - low]).astype(jnp.int32)
    smem, vmem = pl.BlockSpec(memory_space=pltpu.SMEM), pl.BlockSpec(memory_space=pltpu.VMEM)

    def call(kernel, out, scratch, flops, *args):
        return pl.pallas_call(
            kernel,
            out_shape=out,
            in_specs=[smem] + [vmem] * len(args),
            out_specs=jax.tree.map(lambda o: vmem, out),
            scratch_shapes=scratch,
            compiler_params=pltpu.CompilerParams(vmem_limit_bytes=16 << 20),
            cost_estimate=pl.CostEstimate(flops=flops, bytes_accessed=1 << 20, transcendentals=0),
        )(place, *args)

    def square(v, d):
        return lax.ppermute(v, "tp", [(i, i ^ d) for i in range(4)])

    def across(v):
        return lax.ppermute(v, "fsdp", [(i, i ^ 2) for i in range(4)])

    def struct(rows, cols, dtype):
        return jax.ShapeDtypeStruct((rows, cols), dtype)

    def term(v, *parts):
        n = len(v) // 2 * heads
        out = (struct(4 * half, n, F32),) + tuple(struct(half, count * n, BF16) for _, count in parts)
        kernel = functools.partial(term_kernel, tuple(first for first, _ in parts))
        return call(kernel, out, [], n << 20, turned, *v)

    def plus(v, came):
        return (v + came.astype(F32)).astype(BF16)

    def far_plus(v, came):
        n = v.shape[1]
        return jnp.concatenate([plus(v[:half], came[:, :n]), plus(v[half : 2 * half], came[:, n : 2 * n])], 1)

    def back(base, ranks, *weights):
        n = len(ranks) * half
        return call(
            functools.partial(back_kernel, base, ranks),
            (struct(2 * keys, n, BF16), struct(2 * keys, n, F32)),
            [pltpu.VMEM((n, 4 * heads), BF16)], len(ranks) * (3 << 28),
            residual_grad, res_other, v0, vx, vy, vd, v0_other, vx_other, vy_other, vd_other, chosen, *weights,
        )

    got = phase((value_grad, layer_input, residual_grad, value_weight, place, low == 1, end == 1, core * half))
    value_grad, layer_input, residual_grad, value_weight, place, is_low, is_end, first_row = got

    v0 = value_grad
    v0_other, weight_rows = phase((core_swap(v0), value_weight))
    w_own = lax.dynamic_slice_in_dim(weight_rows, first_row, half, 0)
    in_other, res_other = core_swap(layer_input), core_swap(residual_grad)
    w_inner, in_other = phase((w_own, in_other))
    turned = call(turn_kernel, jax.ShapeDtypeStruct((2, 4 * half, tokens), BF16), [], 0, layer_input, in_other)
    term0, send0 = term((v0, v0_other), (0, 4))
    got = phase((outer(w_own), inner(w_inner), square(v0, 1), square(v0, 2), turned, term0, send0,
                 res_other))
    w_beside, w_mid, vx, vy, turned, term0, send0, res_other = got

    vx_other, vy_other = core_swap(vx), core_swap(vy)
    term1, send1, near1 = term((vx, vy, vx_other, vy_other), (0, 2), (2, 1))
    key = owner[:, 0] * keys + key_row
    key_both = jnp.concatenate([key, core_swap(key)])[None, :]
    chosen = call(choose_kernel, struct(4 * keys, 2 * tokens, BF16), [], 0, key_both)
    got = phase((outer(jnp.where(is_end, send0, w_mid)), inner(w_beside), square(v0, 3), term1, send1, near1, chosen))
    i0, w_end, vd, term1, send1, near1, chosen = got
    w_third = i0

    vd_other, sums0 = phase((core_swap(vd), far_plus(term0, i0)))
    b0 = inner(sums0)
    term2, send2, near2 = term((vd, vd_other), (0, 2), (2, 1))
    back0 = plus(term0[2 * half : 3 * half], b0[:, :heads])
    send2 = jnp.where(is_end, send2, jnp.concatenate([back0, back0], 1))
    send_a, keep_a = back(14, (5, 6, 7), w_own, w_beside, w_mid, w_third)
    got = phase((outer(jnp.where(is_end, send1, w_end)), b0, term1, term2, send_a, keep_a, term0, near1, near2, send2))
    i1, b0, term1, term2, send_a, keep_a, term0, near1, near2, send2 = got
    w_fourth = i1

    def joined(a, b):
        return jnp.where(is_low, jnp.concatenate([a, b], 1), jnp.concatenate([b, a], 1))

    i2 = outer(send2)
    send_b, keep_b = back(8, (8,), w_end, w_fourth)
    keep = joined(keep_a, keep_b)
    b1 = inner(far_plus(term1, i1))
    b2 = inner(far_plus(term2, i2))
    got = phase((outer(joined(send_a, send_b)), b1, b2, term0, term1, term2, keep, i2))
    k1, b1, b2, term0, term1, term2, keep, i2 = got

    k2 = across(plus(keep[keys:], k1[keys:]))
    back1 = plus(term1[2 * half : 3 * half], b1[:, : 2 * heads])
    back2 = plus(term2[2 * half : 3 * half], b2[:, :heads])
    i3 = outer(jnp.where(
        is_end, jnp.concatenate([near1, near2], 1), jnp.concatenate([back1, back2], 1)
    ))
    key_half = keep[:keys] + k1[:keys].astype(F32)
    weight_half = jnp.concatenate([
        term0[3 * half :] + jnp.where(is_end, i2[:, :heads], i0[:, 2 * heads : 3 * heads]).astype(F32)
        + b0[:, heads:].astype(F32),
        term1[3 * half :] + b1[:, 2 * heads :].astype(F32),
        term2[3 * half :] + b2[:, heads:].astype(F32),
    ], 1)
    weight_grad, done = call(
        join_weight_kernel, (struct(part, 4 * heads, F32), struct(8, 128, F32)), [], 0,
        weight_half, core_swap(weight_half), i3, core_swap(i3),
    )
    key_grad = call(
        join_key_kernel, struct(keys, features, F32), [], 0,
        done, key_half, core_swap(key_half), k2, core_swap(k2),
    )
    return weight_grad, key_grad


def solution(mesh):
    shape = dict(mesh.shape)
    special = shape == {"dp": 2, "fsdp": 4, "tp": 4}
    return jax.shard_map(
        pair_body if special else general_body,
        mesh=mesh,
        in_specs=(
            P(("dp", "fsdp"), "tp"),
            P(("dp", "fsdp"), "tp"),
            P(("dp", "fsdp"), "tp"),
            P(("tp", "fsdp"), None),
            P(("dp", "fsdp"), None),
            P(("dp", "fsdp")),
        ),
        out_specs=(P(("tp", "fsdp"), None), P("fsdp", "tp")),
        check_vma=False,
    )
```

```python
import functools

import jax
import jax.numpy as jnp
from jax import lax
from jax.experimental import pallas as pl
from jax.experimental.pallas import tpu as pltpu
from jax.sharding import PartitionSpec as P

F32, BF16 = jnp.float32, jnp.bfloat16
KEY_DEV = 256


def dot(a, b, ca, cb):
    return lax.dot_general(a, b, (((ca,), (cb,)), ((), ())), preferred_element_type=F32)


def general_body(layer_input, value_grad, residual_grad, value_weight, owner, key_row):
    all_heads = lax.all_gather(value_grad, "tp", axis=1, tiled=True)
    tok_rows, features = layer_input.shape
    groups = lax.axis_size("fsdp")
    slots = 2 * tok_rows // groups
    keys_here = KEY_DEV
    width = all_heads.shape[1]
    term = dot(layer_input, all_heads, 0, 0)
    pieces = term.astype(BF16).reshape(groups, features // groups, width)
    arrived = lax.all_to_all(pieces, "fsdp", split_axis=0, concat_axis=0, tiled=True)
    shard = jnp.sum(arrived.astype(F32), axis=0)
    back = dot(all_heads, lax.all_gather(value_weight, "fsdp", axis=0, tiled=True), 1, 1)
    input_grad = (residual_grad.astype(F32) + back).astype(BF16)
    target = owner[:, 0]
    onehot = (target[:, None] == jnp.arange(groups, dtype=jnp.int32)[None, :]).astype(jnp.int32)
    position = jnp.sum(jnp.cumsum(onehot, axis=0) * onehot, axis=1) - 1
    place = target * slots + position
    chooser = jnp.arange(groups * slots, dtype=jnp.int32)[:, None] == place[None, :]
    outgoing = dot(chooser.astype(BF16), input_grad, 1, 0).astype(BF16)
    out_keys = jnp.sum(jnp.where(chooser, key_row[None, :] + 1, 0), axis=1) - 1
    arrived = lax.all_to_all(outgoing, "fsdp", split_axis=0, concat_axis=0, tiled=True)
    arrived_keys = lax.all_to_all(out_keys, "fsdp", split_axis=0, concat_axis=0, tiled=True)
    selector = (arrived_keys[:, None] == jnp.arange(keys_here, dtype=jnp.int32)[None, :]).astype(BF16)
    table = dot(selector, arrived, 0, 0)
    return lax.psum(shard, "dp"), lax.psum(table, "dp")


def turn_kernel(place, mine, other, out):
    half = mine.shape[1] // 8
    for side, ref in enumerate((mine, other)):
        for i, rank in enumerate((8, 7, 6, 5)):
            cols = pl.ds(pl.multiple_of((2 * place[rank] + place[4]) * half, half), half)
            out[side, i * half : (i + 1) * half, :] = ref[:, cols].T


def term_kernel(rounded, place, turned, *refs):
    n = sum(r.shape == refs[0].shape for r in refs) // 2
    heads, out, sends = refs[: 2 * n], refs[2 * n], refs[1 + 2 * n :]
    width = heads[0].shape[1]
    for k in range(n):
        cols = slice(k * width, (k + 1) * width)
        out[:, cols] = dot(turned[0], heads[k][...], 1, 0) + dot(turned[1], heads[n + k][...], 1, 0)
    half, wide = out.shape[0] // 4, out.shape[1]
    for first, send in zip(rounded, sends):
        for j in range(send.shape[1] // wide):
            row = (first + j) * half
            send[:, j * wide : (j + 1) * wide] = out[row : row + half, :].astype(BF16)


def choose_kernel(place, key, out):
    keys = out.shape[0] // 4
    row = lax.broadcasted_iota(jnp.int32, (keys, key.shape[1]), 0)
    for j in range(4):
        hit = row + place[10 + j] * keys == key[...]
        out[j * keys : (j + 1) * keys, :] = jnp.where(hit, 1.0, 0.0).astype(BF16)


def back_kernel(base, ranks, place, *refs):
    residuals, heads, chosen, weights, (send, keep, weight) = refs[:2], refs[2:10], refs[10], refs[11:-3], refs[-3:]
    half, width = weights[0].shape[0], heads[0].shape[1]
    tokens = heads[0].shape[0]
    first = place[base]

    def put(rank, ref):
        weight[pl.ds(pl.multiple_of((place[rank] - first) * half, half), half), :] = ref[...]

    for rank, ref in zip(ranks[:-1], weights):
        put(rank, ref)
    for here in range(2):
        pl.when(place[9] == here)(lambda here=here: put(ranks[-1], weights[len(ranks) - 1 + here]))

    total = [None] * 2
    starts = [pl.multiple_of((2 * (first + p) + place[4]) * half, half) for p in range(len(ranks))]
    for side in range(2):
        acc = jnp.concatenate([residuals[side][:, pl.ds(at, half)] for at in starts], 1).astype(F32)
        for k in range(4):
            cols = pl.ds(pl.multiple_of(place[k] * width, width), width)
            acc = acc + dot(heads[4 * side + k][...], weight[:, cols], 1, 1)
        rows = acc.astype(BF16)
        for i in range(2):
            size = send.shape[0]
            pick = chosen[i * size : (i + 1) * size, side * tokens : (side + 1) * tokens]
            add = dot(pick, rows, 1, 0)
            total[i] = add if side == 0 else total[i] + add
    send[...] = total[0].astype(BF16)
    keep[...] = total[1]


def join_weight_kernel(place, mine, pair, last, last_pair, out, done):
    half, width = mine.shape[0], mine.shape[1] // 4
    here = pl.multiple_of(place[4] * half, half)
    there = pl.multiple_of(half - place[4] * half, half)
    for at, kept, came in ((here, mine, last), (there, pair, last_pair)):
        for k in range(4):
            start = pl.multiple_of(place[k] * width, width)
            value = kept[:, k * width : (k + 1) * width]
            if k > 0:
                value = value + came[:, (k - 1) * width : k * width].astype(F32)
            out[pl.ds(at, half), pl.ds(start, width)] = value
    done[...] = jnp.zeros_like(done)


def join_key_kernel(place, before, mine, pair, last, last_pair, out):
    first = place[4] == 0
    half = mine.shape[1] // 4
    for p in range(4):
        cols = slice(p * half, (p + 1) * half)
        a = mine[:, cols] + last[:, cols].astype(F32)
        b = pair[:, cols] + last_pair[:, cols].astype(F32)
        out[:, 2 * p * half : (2 * p + 1) * half] = jnp.where(first, a, b)
        out[:, (2 * p + 1) * half : (2 * p + 2) * half] = jnp.where(first, b, a)


def pair_body(layer_input, value_grad, residual_grad, value_weight, owner, key_row):
    core, z, t = (lax.axis_index(n) for n in ("dp", "fsdp", "tp"))
    tokens, features = layer_input.shape
    heads = value_grad.shape[1]
    part = features // 4
    half = part // 2
    keys = KEY_DEV
    phase = lax.optimization_barrier

    def core_swap(v):
        return lax.ppermute(v, "dp", [(0, 1), (1, 0)])

    def outer(v):
        return lax.ppermute(v, "fsdp", [(0, 1), (1, 0), (2, 3), (3, 2)])

    def inward(v):
        return lax.ppermute(v, "fsdp", [(0, 1), (3, 2)])

    def outward(v):
        return lax.ppermute(v, "fsdp", [(1, 0), (2, 3)])

    def inner(v):
        return lax.ppermute(v, "fsdp", [(1, 2), (2, 1)])

    end = ((z == 0) | (z == 3)).astype(jnp.int32)
    low = (z < 2).astype(jnp.int32)
    beside = z ^ 1
    far_mid = 1 + low
    far_end = 3 * low
    place = jnp.stack([t, t ^ 1, t ^ 2, t ^ 3, core, z, beside, far_mid, far_end, end, z ^ 1, z ^ 3, z, z ^ 2, 1 - low]).astype(jnp.int32)
    smem, vmem = pl.BlockSpec(memory_space=pltpu.SMEM), pl.BlockSpec(memory_space=pltpu.VMEM)

    def call(kernel, out, scratch, flops, *args):
        return pl.pallas_call(
            kernel,
            out_shape=out,
            in_specs=[smem] + [vmem] * len(args),
            out_specs=jax.tree.map(lambda o: vmem, out),
            scratch_shapes=scratch,
            compiler_params=pltpu.CompilerParams(vmem_limit_bytes=16 << 20),
            cost_estimate=pl.CostEstimate(flops=flops, bytes_accessed=(1 << 20) if flops else 0, transcendentals=0),
        )(place, *args)

    def square(v, d):
        return lax.ppermute(v, "tp", [(i, i ^ d) for i in range(4)])

    def across(v):
        return lax.ppermute(v, "fsdp", [(i, i ^ 2) for i in range(4)])

    def struct(rows, cols, dtype):
        return jax.ShapeDtypeStruct((rows, cols), dtype)

    def term(v, *parts):
        n = len(v) // 2 * heads
        out = (struct(4 * half, n, F32),) + tuple(struct(half, count * n, BF16) for _, count in parts)
        kernel = functools.partial(term_kernel, tuple(first for first, _ in parts))
        return call(kernel, out, [], 0, turned, *v)

    def plus(v, came):
        return (v + came.astype(F32)).astype(BF16)

    def far_plus(v, came):
        n = v.shape[1]
        return jnp.concatenate([plus(v[:half], came[:, :n]), plus(v[half : 2 * half], came[:, n : 2 * n])], 1)

    def back(base, ranks, *weights):
        n = len(ranks) * half
        return call(
            functools.partial(back_kernel, base, ranks),
            (struct(2 * keys, n, BF16), struct(2 * keys, n, F32)),
            [pltpu.VMEM((n, 4 * heads), BF16)], len(ranks) * (3 << 29),
            residual_grad, res_other, v0, vx, vy, vd, v0_other, vx_other, vy_other, vd_other, chosen, *weights,
        )

    got = phase((value_grad, layer_input, residual_grad, value_weight, place, low == 1, end == 1, core * half))
    value_grad, layer_input, residual_grad, value_weight, place, is_low, is_end, first_row = got

    v0 = value_grad
    v0_other, weight_rows = phase((core_swap(v0), value_weight))
    w_own = lax.dynamic_slice_in_dim(weight_rows, first_row, half, 0)
    in_other, res_other = core_swap(layer_input), core_swap(residual_grad)
    w_inner, in_other = phase((w_own, in_other))
    turned = call(turn_kernel, jax.ShapeDtypeStruct((2, 4 * half, tokens), BF16), [], 0, layer_input, in_other)
    term0, send0 = term((v0, v0_other), (0, 4))
    w_beside = outer(w_own)
    got = phase((inner(w_inner), square(v0, 1), square(v0, 2), turned, term0, send0, res_other))
    w_mid, vx, vy, turned, term0, send0, res_other = got

    vx_other, vy_other = core_swap(vx), core_swap(vy)
    term1, send1, near1 = term((vx, vy, vx_other, vy_other), (0, 2), (2, 1))
    key = owner[:, 0] * keys + key_row
    key_both = jnp.concatenate([key, core_swap(key)])[None, :]
    chosen = call(choose_kernel, struct(4 * keys, 2 * tokens, BF16), [], 0, key_both)
    i0 = outer(jnp.where(is_end, send0, w_mid))
    got = phase((inner(w_beside), square(v0, 3), term1, send1, near1, chosen))
    w_end, vd, term1, send1, near1, chosen = got
    w_third = i0

    vd_other, sums0 = phase((core_swap(vd), far_plus(term0, i0)))
    b0 = inner(sums0)
    term2, send2, near2 = term((vd, vd_other), (0, 2), (2, 1))
    back0 = plus(term0[2 * half : 3 * half], b0[:, :heads])
    send2 = jnp.where(is_end, send2, jnp.concatenate([back0, back0], 1))
    send_a, keep_a = back(14, (5, 6, 7), w_own, w_beside, w_mid, w_third)
    got = phase((outer(jnp.where(is_end, send1, w_end)), b0, term1, term2, send_a, keep_a, term0, near1, near2, send2))
    i1, b0, term1, term2, send_a, keep_a, term0, near1, near2, send2 = got
    w_fourth = i1

    def joined(a, b):
        return jnp.where(is_low, jnp.concatenate([a, b], 1), jnp.concatenate([b, a], 1))

    i2 = outer(send2)
    send_b, keep_b = back(8, (8,), w_end, w_fourth)
    keep = joined(keep_a, keep_b)
    b1 = inner(far_plus(term1, i1))
    b2 = inner(far_plus(term2, i2))
    got = phase((outer(joined(send_a, send_b)), b1, b2, term0, term1, term2, keep, i2))
    k1, b1, b2, term0, term1, term2, keep, i2 = got

    k2 = across(plus(keep[keys:], k1[keys:]))
    back1 = plus(term1[2 * half : 3 * half], b1[:, : 2 * heads])
    back2 = plus(term2[2 * half : 3 * half], b2[:, :heads])
    i3 = outer(jnp.where(
        is_end, jnp.concatenate([near1, near2], 1), jnp.concatenate([back1, back2], 1)
    ))
    key_half = keep[:keys] + k1[:keys].astype(F32)
    weight_half = jnp.concatenate([
        term0[3 * half :] + jnp.where(is_end, i2[:, :heads], i0[:, 2 * heads : 3 * heads]).astype(F32)
        + b0[:, heads:].astype(F32),
        term1[3 * half :] + b1[:, 2 * heads :].astype(F32),
        term2[3 * half :] + b2[:, heads:].astype(F32),
    ], 1)
    weight_grad, done = call(
        join_weight_kernel, (struct(part, 4 * heads, F32), struct(8, 128, F32)), [], 0,
        weight_half, core_swap(weight_half), i3, core_swap(i3),
    )
    key_grad = call(
        join_key_kernel, struct(keys, features, F32), [], 0,
        done, key_half, core_swap(key_half), k2, core_swap(k2),
    )
    return weight_grad, key_grad


def solution(mesh):
    shape = dict(mesh.shape)
    special = shape == {"dp": 2, "fsdp": 4, "tp": 4}
    return jax.shard_map(
        pair_body if special else general_body,
        mesh=mesh,
        in_specs=(
            P(("dp", "fsdp"), "tp"),
            P(("dp", "fsdp"), "tp"),
            P(("dp", "fsdp"), "tp"),
            P(("tp", "fsdp"), None),
            P(("dp", "fsdp"), None),
            P(("dp", "fsdp")),
        ),
        out_specs=(P(("tp", "fsdp"), None), P("fsdp", "tp")),
        check_vma=False,
    )
```

```python
import functools

import jax
import jax.numpy as jnp
from jax import lax
from jax.experimental import pallas as pl
from jax.experimental.pallas import tpu as pltpu
from jax.sharding import PartitionSpec as P

F32, BF16 = jnp.float32, jnp.bfloat16
KEY_DEV = 256


def dot(a, b, ca, cb):
    return lax.dot_general(a, b, (((ca,), (cb,)), ((), ())), preferred_element_type=F32)


def general_body(layer_input, value_grad, residual_grad, value_weight, owner, key_row):
    all_heads = lax.all_gather(value_grad, "tp", axis=1, tiled=True)
    tok_rows, features = layer_input.shape
    groups = lax.axis_size("fsdp")
    slots = 2 * tok_rows // groups
    keys_here = KEY_DEV
    width = all_heads.shape[1]
    term = dot(layer_input, all_heads, 0, 0)
    pieces = term.astype(BF16).reshape(groups, features // groups, width)
    arrived = lax.all_to_all(pieces, "fsdp", split_axis=0, concat_axis=0, tiled=True)
    shard = jnp.sum(arrived.astype(F32), axis=0)
    back = dot(all_heads, lax.all_gather(value_weight, "fsdp", axis=0, tiled=True), 1, 1)
    input_grad = (residual_grad.astype(F32) + back).astype(BF16)
    target = owner[:, 0]
    onehot = (target[:, None] == jnp.arange(groups, dtype=jnp.int32)[None, :]).astype(jnp.int32)
    position = jnp.sum(jnp.cumsum(onehot, axis=0) * onehot, axis=1) - 1
    place = target * slots + position
    chooser = jnp.arange(groups * slots, dtype=jnp.int32)[:, None] == place[None, :]
    outgoing = dot(chooser.astype(BF16), input_grad, 1, 0).astype(BF16)
    out_keys = jnp.sum(jnp.where(chooser, key_row[None, :] + 1, 0), axis=1) - 1
    arrived = lax.all_to_all(outgoing, "fsdp", split_axis=0, concat_axis=0, tiled=True)
    arrived_keys = lax.all_to_all(out_keys, "fsdp", split_axis=0, concat_axis=0, tiled=True)
    selector = (arrived_keys[:, None] == jnp.arange(keys_here, dtype=jnp.int32)[None, :]).astype(BF16)
    table = dot(selector, arrived, 0, 0)
    return lax.psum(shard, "dp"), lax.psum(table, "dp")


def turn_kernel(place, mine, other, out):
    half = mine.shape[1] // 8
    for side, ref in enumerate((mine, other)):
        for i, rank in enumerate((8, 7, 6, 5)):
            cols = pl.ds(pl.multiple_of((2 * place[rank] + place[4]) * half, half), half)
            out[side, i * half : (i + 1) * half, :] = ref[:, cols].T


def term_kernel(rounded, place, turned, *refs):
    n = sum(r.shape == refs[0].shape for r in refs) // 2
    heads, out, sends = refs[: 2 * n], refs[2 * n], refs[1 + 2 * n :]
    width = heads[0].shape[1]
    for k in range(n):
        cols = slice(k * width, (k + 1) * width)
        out[:, cols] = dot(turned[0], heads[k][...], 1, 0) + dot(turned[1], heads[n + k][...], 1, 0)
    half, wide = out.shape[0] // 4, out.shape[1]
    for first, send in zip(rounded, sends):
        for j in range(send.shape[1] // wide):
            row = (first + j) * half
            send[:, j * wide : (j + 1) * wide] = out[row : row + half, :].astype(BF16)


def choose_kernel(place, key, out):
    keys = out.shape[0] // 4
    row = lax.broadcasted_iota(jnp.int32, (keys, key.shape[1]), 0)
    for j in range(4):
        hit = row + place[10 + j] * keys == key[...]
        out[j * keys : (j + 1) * keys, :] = jnp.where(hit, 1.0, 0.0).astype(BF16)


def back_rows(place, first, count, weight, residuals, heads, chosen, send, keep):
    half = weight.shape[0] // count
    tokens, width = heads[0].shape
    total = [None] * 2
    starts = [pl.multiple_of((2 * (first + p) + place[4]) * half, half) for p in range(count)]
    for side in range(2):
        acc = jnp.concatenate([residuals[side][:, pl.ds(at, half)] for at in starts], 1).astype(F32)
        for k in range(4):
            cols = pl.ds(pl.multiple_of(place[k] * width, width), width)
            acc = acc + dot(heads[4 * side + k][...], weight[:, cols], 1, 1)
        rows = acc.astype(BF16)
        for i in range(2):
            size = send.shape[0]
            pick = chosen[i * size : (i + 1) * size, side * tokens : (side + 1) * tokens]
            add = dot(pick, rows, 1, 0)
            total[i] = add if side == 0 else total[i] + add
    send[...] = total[0].astype(BF16)
    keep[...] = total[1]


def back_kernel(place, *refs):
    residuals, heads, chosen, refs = refs[:2], refs[2:10], refs[10], refs[11:]
    own, beside, mid, third, end, send, keep, send_mid, keep_mid, weight = refs
    half = own.shape[0]
    first = place[14]

    def put(rank, ref):
        weight[pl.ds(pl.multiple_of((place[rank] - first) * half, half), half), :] = ref[...]

    put(5, own)
    put(6, beside)
    pl.when(place[9] == 0)(lambda: put(7, mid))
    pl.when(place[9] == 1)(lambda: put(7, third))
    back_rows(place, first, 3, weight, residuals, heads, chosen, send, keep)
    pl.when(place[9] == 0)(
        lambda: back_rows(place, place[8], 1, end, residuals, heads, chosen, send_mid, keep_mid)
    )


def back_end_kernel(place, *refs):
    residuals, heads, chosen, (fourth, send_mid, keep_mid, send, keep) = refs[:2], refs[2:10], refs[10], refs[11:]

    @pl.when(place[9] == 0)
    def _():
        send[...] = send_mid[...]
        keep[...] = keep_mid[...]

    pl.when(place[9] == 1)(lambda: back_rows(place, place[8], 1, fourth, residuals, heads, chosen, send, keep))


def join_kernel(place, mine, pair, last, last_pair, key_mine, key_pair, key_last, key_last_pair,
                out, key_out, joined, key_joined, sems):
    half, width = mine.shape[0], mine.shape[1] // 4
    copies = []
    for side in range(2):
        here = place[4] == side
        rows = pl.ds(side * half, half)
        for k in range(4):
            cols = slice(k * width, (k + 1) * width)
            value = jnp.where(here, mine[:, cols], pair[:, cols])
            if k > 0:
                came = slice((k - 1) * width, k * width)
                value = value + jnp.where(here, last[:, came], last_pair[:, came]).astype(F32)
            joined[rows, pl.ds(pl.multiple_of(place[k] * width, width), width)] = value
        copies.append(pltpu.make_async_copy(joined.at[rows], out.at[rows], sems.at[side]))
        copies[-1].start()
    size, high = key_mine.shape[1] // 4, key_mine.shape[0] // 2
    first = place[4] == 0
    for part in range(2):
        rows = pl.ds(part * high, high)
        for p in range(4):
            cols = slice(p * size, (p + 1) * size)
            a = key_mine[rows, cols] + key_last[rows, cols].astype(F32)
            b = key_pair[rows, cols] + key_last_pair[rows, cols].astype(F32)
            key_joined[rows, 2 * p * size : (2 * p + 1) * size] = jnp.where(first, a, b)
            key_joined[rows, (2 * p + 1) * size : (2 * p + 2) * size] = jnp.where(first, b, a)
        copies.append(pltpu.make_async_copy(key_joined.at[rows], key_out.at[rows], sems.at[2 + part]))
        copies[-1].start()
    for copy in copies:
        copy.wait()


def pair_body(layer_input, value_grad, residual_grad, value_weight, owner, key_row):
    core, z, t = (lax.axis_index(n) for n in ("dp", "fsdp", "tp"))
    tokens, features = layer_input.shape
    heads = value_grad.shape[1]
    part = features // 4
    half = part // 2
    keys = KEY_DEV
    phase = lax.optimization_barrier

    def core_swap(v):
        return lax.ppermute(v, "dp", [(0, 1), (1, 0)])

    def outer(v):
        return lax.ppermute(v, "fsdp", [(0, 1), (1, 0), (2, 3), (3, 2)])

    def inward(v):
        return lax.ppermute(v, "fsdp", [(0, 1), (3, 2)])

    def outward(v):
        return lax.ppermute(v, "fsdp", [(1, 0), (2, 3)])

    def inner(v):
        return lax.ppermute(v, "fsdp", [(1, 2), (2, 1)])

    end = ((z == 0) | (z == 3)).astype(jnp.int32)
    low = (z < 2).astype(jnp.int32)
    beside = z ^ 1
    far_mid = 1 + low
    far_end = 3 * low
    place = jnp.stack([t, t ^ 1, t ^ 2, t ^ 3, core, z, beside, far_mid, far_end, end, z ^ 1, z ^ 3, z, z ^ 2, 1 - low]).astype(jnp.int32)
    smem, vmem = pl.BlockSpec(memory_space=pltpu.SMEM), pl.BlockSpec(memory_space=pltpu.VMEM)

    def call(kernel, out, scratch, flops, *args):
        return pl.pallas_call(
            kernel,
            out_shape=out,
            in_specs=[smem] + [vmem] * len(args),
            out_specs=jax.tree.map(lambda o: vmem, out),
            scratch_shapes=scratch,
            compiler_params=pltpu.CompilerParams(vmem_limit_bytes=16 << 20),
            cost_estimate=pl.CostEstimate(flops=flops, bytes_accessed=(1 << 20) if flops else 0, transcendentals=0),
        )(place, *args)

    def square(v, d):
        return lax.ppermute(v, "tp", [(i, i ^ d) for i in range(4)])

    def across(v):
        return lax.ppermute(v, "fsdp", [(i, i ^ 2) for i in range(4)])

    def struct(rows, cols, dtype):
        return jax.ShapeDtypeStruct((rows, cols), dtype)

    def term(v, *parts):
        n = len(v) // 2 * heads
        out = (struct(4 * half, n, F32),) + tuple(struct(half, count * n, BF16) for _, count in parts)
        kernel = functools.partial(term_kernel, tuple(first for first, _ in parts))
        return call(kernel, out, [], {1: 0, 3: 0}.get(len(v) // 2 + len(parts) - 1, 0), turned, *v)

    def plus(v, came):
        return (v + came.astype(F32)).astype(BF16)

    def far_plus(v, came):
        n = v.shape[1]
        return jnp.concatenate([plus(v[:half], came[:, :n]), plus(v[half : 2 * half], came[:, n : 2 * n])], 1)

    def back(kernel, parts, cost, scratch, *refs):
        out = [struct(2 * keys, n * half, kind) for n in parts for kind in (BF16, F32)]
        return call(
            kernel, out, scratch, cost, residual_grad, res_other,
            v0, vx, vy, vd, v0_other, vx_other, vy_other, vd_other, chosen, *refs,
        )

    got = phase((value_grad, layer_input, residual_grad, value_weight, place, low == 1, end == 1, core * half))
    value_grad, layer_input, residual_grad, value_weight, place, is_low, is_end, first_row = got

    v0 = value_grad
    v0_other, weight_rows = phase((core_swap(v0), value_weight))
    w_own = lax.dynamic_slice_in_dim(weight_rows, first_row, half, 0)
    in_other, res_other = core_swap(layer_input), core_swap(residual_grad)
    w_inner, in_other = phase((w_own, in_other))
    turned = call(turn_kernel, jax.ShapeDtypeStruct((2, 4 * half, tokens), BF16), [], 1073741824, layer_input, in_other)
    term0, send0 = term((v0, v0_other), (0, 4))
    w_beside = outer(w_own)
    got = phase((inner(w_inner), square(v0, 1), square(v0, 2), turned, term0, send0, res_other))
    w_mid, vx, vy, turned, term0, send0, res_other = got

    vx_other, vy_other = core_swap(vx), core_swap(vy)
    term1, send1, near1 = term((vx, vy, vx_other, vy_other), (0, 2), (2, 1))
    key = owner[:, 0] * keys + key_row
    key_both = jnp.concatenate([key, core_swap(key)])[None, :]
    chosen = call(choose_kernel, struct(4 * keys, 2 * tokens, BF16), [], 0, key_both)
    i0 = outer(jnp.where(is_end, send0, w_mid))
    got = phase((inner(w_beside), square(v0, 3), term1, send1, near1, chosen))
    w_end, vd, term1, send1, near1, chosen = got
    w_third = i0

    vd_other, sums0 = phase((core_swap(vd), far_plus(term0, i0)))
    b0 = inner(sums0)
    term2, send2, near2 = term((vd, vd_other), (0, 2), (2, 1))
    back0 = plus(term0[2 * half : 3 * half], b0[:, :heads])
    send2 = jnp.where(is_end, send2, jnp.concatenate([back0, back0], 1))
    send_a, keep_a, send_mid, keep_mid = back(
        back_kernel, (3, 1), 4831838208, [pltpu.VMEM((3 * half, 4 * heads), BF16)],
        w_own, w_beside, w_mid, w_third, w_end,
    )
    got = phase((outer(jnp.where(is_end, send1, w_end)), b0, term1, term2, send_a, keep_a, term0, near1, near2, send2))
    i1, b0, term1, term2, send_a, keep_a, term0, near1, near2, send2 = got
    w_fourth = i1

    def joined(a, b):
        return jnp.where(is_low, jnp.concatenate([a, b], 1), jnp.concatenate([b, a], 1))

    i2 = outer(send2)
    send_b, keep_b = back(back_end_kernel, (1,), 4294967296, [], w_fourth, send_mid, keep_mid)
    keep = joined(keep_a, keep_b)
    b1 = inner(far_plus(term1, i1))
    b2 = inner(far_plus(term2, i2))
    got = phase((outer(joined(send_a, send_b)), b1, b2, term0, term1, term2, keep, i2))
    k1, b1, b2, term0, term1, term2, keep, i2 = got

    k2 = across(plus(keep[keys:], k1[keys:]))
    back1 = plus(term1[2 * half : 3 * half], b1[:, : 2 * heads])
    back2 = plus(term2[2 * half : 3 * half], b2[:, :heads])
    i3 = outer(jnp.where(
        is_end, jnp.concatenate([near1, near2], 1), jnp.concatenate([back1, back2], 1)
    ))
    key_half = keep[:keys] + k1[:keys].astype(F32)
    weight_half = jnp.concatenate([
        term0[3 * half :] + jnp.where(is_end, i2[:, :heads], i0[:, 2 * heads : 3 * heads]).astype(F32)
        + b0[:, heads:].astype(F32),
        term1[3 * half :] + b1[:, 2 * heads :].astype(F32),
        term2[3 * half :] + b2[:, heads:].astype(F32),
    ], 1)
    outs = (struct(part, 4 * heads, F32), struct(keys, features, F32))
    return tuple(pl.pallas_call(
        join_kernel,
        out_shape=outs,
        in_specs=[smem] + [vmem] * 8,
        out_specs=(pl.BlockSpec(memory_space=pl.ANY),) * 2,
        scratch_shapes=[pltpu.VMEM(o.shape, F32) for o in outs] + [pltpu.SemaphoreType.DMA((4,))],
        compiler_params=pltpu.CompilerParams(vmem_limit_bytes=16 << 20),
        cost_estimate=pl.CostEstimate(flops=0, bytes_accessed=1 << 20, transcendentals=0),
    )(place, weight_half, core_swap(weight_half), i3, core_swap(i3), key_half, core_swap(key_half), k2, core_swap(k2)))


def solution(mesh):
    shape = dict(mesh.shape)
    special = shape == {"dp": 2, "fsdp": 4, "tp": 4}
    return jax.shard_map(
        pair_body if special else general_body,
        mesh=mesh,
        in_specs=(
            P(("dp", "fsdp"), "tp"),
            P(("dp", "fsdp"), "tp"),
            P(("dp", "fsdp"), "tp"),
            P(("tp", "fsdp"), None),
            P(("dp", "fsdp"), None),
            P(("dp", "fsdp")),
        ),
        out_specs=(P(("tp", "fsdp"), None), P("fsdp", "tp")),
        check_vma=False,
    )
```

```python
import functools

import jax
import jax.numpy as jnp
from jax import lax
from jax.experimental import pallas as pl
from jax.experimental.pallas import tpu as pltpu
from jax.sharding import PartitionSpec as P

F32, BF16 = jnp.float32, jnp.bfloat16
KEY_DEV = 256


def dot(a, b, ca, cb):
    return lax.dot_general(a, b, (((ca,), (cb,)), ((), ())), preferred_element_type=F32)


def general_body(layer_input, value_grad, residual_grad, value_weight, owner, key_row):
    all_heads = lax.all_gather(value_grad, "tp", axis=1, tiled=True)
    tok_rows, features = layer_input.shape
    groups = lax.axis_size("fsdp")
    slots = 2 * tok_rows // groups
    keys_here = KEY_DEV
    width = all_heads.shape[1]
    term = dot(layer_input, all_heads, 0, 0)
    pieces = term.astype(BF16).reshape(groups, features // groups, width)
    arrived = lax.all_to_all(pieces, "fsdp", split_axis=0, concat_axis=0, tiled=True)
    shard = jnp.sum(arrived.astype(F32), axis=0)
    back = dot(all_heads, lax.all_gather(value_weight, "fsdp", axis=0, tiled=True), 1, 1)
    input_grad = (residual_grad.astype(F32) + back).astype(BF16)
    target = owner[:, 0]
    onehot = (target[:, None] == jnp.arange(groups, dtype=jnp.int32)[None, :]).astype(jnp.int32)
    position = jnp.sum(jnp.cumsum(onehot, axis=0) * onehot, axis=1) - 1
    place = target * slots + position
    chooser = jnp.arange(groups * slots, dtype=jnp.int32)[:, None] == place[None, :]
    outgoing = dot(chooser.astype(BF16), input_grad, 1, 0).astype(BF16)
    out_keys = jnp.sum(jnp.where(chooser, key_row[None, :] + 1, 0), axis=1) - 1
    arrived = lax.all_to_all(outgoing, "fsdp", split_axis=0, concat_axis=0, tiled=True)
    arrived_keys = lax.all_to_all(out_keys, "fsdp", split_axis=0, concat_axis=0, tiled=True)
    selector = (arrived_keys[:, None] == jnp.arange(keys_here, dtype=jnp.int32)[None, :]).astype(BF16)
    table = dot(selector, arrived, 0, 0)
    return lax.psum(shard, "dp"), lax.psum(table, "dp")


def turn_kernel(place, mine, other, out):
    half = mine.shape[1] // 8
    for side, ref in enumerate((mine, other)):
        for i, rank in enumerate((8, 7, 6, 5)):
            cols = pl.ds(pl.multiple_of((2 * place[rank] + place[4]) * half, half), half)
            out[side, i * half : (i + 1) * half, :] = ref[:, cols].T


def term_kernel(rounded, place, turned, *refs):
    n = sum(r.shape == refs[0].shape for r in refs) // 2
    heads, out, sends = refs[: 2 * n], refs[2 * n], refs[1 + 2 * n :]
    width = heads[0].shape[1]
    for k in range(n):
        cols = slice(k * width, (k + 1) * width)
        out[:, cols] = dot(turned[0], heads[k][...], 1, 0) + dot(turned[1], heads[n + k][...], 1, 0)
    half, wide = out.shape[0] // 4, out.shape[1]
    for first, send in zip(rounded, sends):
        for j in range(send.shape[1] // wide):
            row = (first + j) * half
            send[:, j * wide : (j + 1) * wide] = out[row : row + half, :].astype(BF16)


def choose_kernel(place, key, out):
    keys = out.shape[0] // 4
    row = lax.broadcasted_iota(jnp.int32, (keys, key.shape[1]), 0)
    for j in range(4):
        hit = row + place[10 + j] * keys == key[...]
        out[j * keys : (j + 1) * keys, :] = jnp.where(hit, 1.0, 0.0).astype(BF16)


def back_rows(place, first, count, weight, residuals, heads, chosen, send, keep):
    half = weight.shape[0] // count
    tokens, width = heads[0].shape
    total = [None] * 2
    starts = [pl.multiple_of((2 * (first + p) + place[4]) * half, half) for p in range(count)]
    for side in range(2):
        acc = jnp.concatenate([residuals[side][:, pl.ds(at, half)] for at in starts], 1).astype(F32)
        for k in range(4):
            cols = pl.ds(pl.multiple_of(place[k] * width, width), width)
            acc = acc + dot(heads[4 * side + k][...], weight[:, cols], 1, 1)
        rows = acc.astype(BF16)
        for i in range(2):
            size = send.shape[0]
            pick = chosen[i * size : (i + 1) * size, side * tokens : (side + 1) * tokens]
            add = dot(pick, rows, 1, 0)
            total[i] = add if side == 0 else total[i] + add
    send[...] = total[0].astype(BF16)
    keep[...] = total[1]


def back_kernel(place, *refs):
    residuals, heads, chosen, refs = refs[:2], refs[2:10], refs[10], refs[11:]
    own, beside, mid, third, end, send, keep, send_mid, keep_mid, weight = refs
    half = own.shape[0]
    first = place[14]

    def put(rank, ref):
        weight[pl.ds(pl.multiple_of((place[rank] - first) * half, half), half), :] = ref[...]

    put(5, own)
    put(6, beside)
    pl.when(place[9] == 0)(lambda: put(7, mid))
    pl.when(place[9] == 1)(lambda: put(7, third))
    back_rows(place, first, 3, weight, residuals, heads, chosen, send, keep)
    pl.when(place[9] == 0)(
        lambda: back_rows(place, place[8], 1, end, residuals, heads, chosen, send_mid, keep_mid)
    )


def back_end_kernel(place, *refs):
    residuals, heads, chosen, (fourth, send_mid, keep_mid, send, keep) = refs[:2], refs[2:10], refs[10], refs[11:]

    @pl.when(place[9] == 0)
    def _():
        send[...] = send_mid[...]
        keep[...] = keep_mid[...]

    pl.when(place[9] == 1)(lambda: back_rows(place, place[8], 1, fourth, residuals, heads, chosen, send, keep))


def join_kernel(place, mine, pair, last, last_pair, key_mine, key_pair, key_last, key_last_pair,
                out, key_out, joined, key_joined, sems):
    half, width = mine.shape[0], mine.shape[1] // 4
    copies = []
    for side in range(2):
        here = place[4] == side
        rows = pl.ds(side * half, half)
        for k in range(4):
            cols = slice(k * width, (k + 1) * width)
            value = jnp.where(here, mine[:, cols], pair[:, cols])
            if k > 0:
                came = slice((k - 1) * width, k * width)
                value = value + jnp.where(here, last[:, came], last_pair[:, came]).astype(F32)
            joined[rows, pl.ds(pl.multiple_of(place[k] * width, width), width)] = value
        copies.append(pltpu.make_async_copy(joined.at[rows], out.at[rows], sems.at[side]))
        copies[-1].start()
    size, high = key_mine.shape[1] // 4, key_mine.shape[0] // 2
    first = place[4] == 0
    for part in range(2):
        rows = pl.ds(part * high, high)
        for p in range(4):
            cols = slice(p * size, (p + 1) * size)
            a = key_mine[rows, cols] + key_last[rows, cols].astype(F32)
            b = key_pair[rows, cols] + key_last_pair[rows, cols].astype(F32)
            key_joined[rows, 2 * p * size : (2 * p + 1) * size] = jnp.where(first, a, b)
            key_joined[rows, (2 * p + 1) * size : (2 * p + 2) * size] = jnp.where(first, b, a)
        copies.append(pltpu.make_async_copy(key_joined.at[rows], key_out.at[rows], sems.at[2 + part]))
        copies[-1].start()
    for copy in copies:
        copy.wait()


def pair_body(layer_input, value_grad, residual_grad, value_weight, owner, key_row):
    core, z, t = (lax.axis_index(n) for n in ("dp", "fsdp", "tp"))
    tokens, features = layer_input.shape
    heads = value_grad.shape[1]
    part = features // 4
    half = part // 2
    keys = KEY_DEV
    phase = lax.optimization_barrier

    def core_swap(v):
        return lax.ppermute(v, "dp", [(0, 1), (1, 0)])

    def outer(v):
        return lax.ppermute(v, "fsdp", [(0, 1), (1, 0), (2, 3), (3, 2)])

    def inward(v):
        return lax.ppermute(v, "fsdp", [(0, 1), (3, 2)])

    def outward(v):
        return lax.ppermute(v, "fsdp", [(1, 0), (2, 3)])

    def inner(v):
        return lax.ppermute(v, "fsdp", [(1, 2), (2, 1)])

    end = ((z == 0) | (z == 3)).astype(jnp.int32)
    low = (z < 2).astype(jnp.int32)
    beside = z ^ 1
    far_mid = 1 + low
    far_end = 3 * low
    place = jnp.stack([t, t ^ 1, t ^ 2, t ^ 3, core, z, beside, far_mid, far_end, end, z ^ 1, z ^ 3, z, z ^ 2, 1 - low]).astype(jnp.int32)
    smem, vmem = pl.BlockSpec(memory_space=pltpu.SMEM), pl.BlockSpec(memory_space=pltpu.VMEM)

    def call(kernel, out, scratch, flops, *args):
        return pl.pallas_call(
            kernel,
            out_shape=out,
            in_specs=[smem] + [vmem] * len(args),
            out_specs=jax.tree.map(lambda o: vmem, out),
            scratch_shapes=scratch,
            compiler_params=pltpu.CompilerParams(vmem_limit_bytes=16 << 20),
            cost_estimate=pl.CostEstimate(flops=flops, bytes_accessed=(1 << 20) if flops else 0, transcendentals=0),
        )(place, *args)

    def square(v, d):
        return lax.ppermute(v, "tp", [(i, i ^ d) for i in range(4)])

    def across(v):
        return lax.ppermute(v, "fsdp", [(i, i ^ 2) for i in range(4)])

    def struct(rows, cols, dtype):
        return jax.ShapeDtypeStruct((rows, cols), dtype)

    def term(v, *parts):
        n = len(v) // 2 * heads
        out = (struct(4 * half, n, F32),) + tuple(struct(half, count * n, BF16) for _, count in parts)
        kernel = functools.partial(term_kernel, tuple(first for first, _ in parts))
        return call(kernel, out, [], (2 << 30) if len(v) == len(parts) == 2 else 0, turned, *v)

    def plus(v, came):
        return (v + came.astype(F32)).astype(BF16)

    def far_plus(v, came):
        n = v.shape[1]
        return jnp.concatenate([plus(v[:half], came[:, :n]), plus(v[half : 2 * half], came[:, n : 2 * n])], 1)

    def back(kernel, parts, cost, scratch, *refs):
        out = [struct(2 * keys, n * half, kind) for n in parts for kind in (BF16, F32)]
        return call(
            kernel, out, scratch, cost, residual_grad, res_other,
            v0, vx, vy, vd, v0_other, vx_other, vy_other, vd_other, chosen, *refs,
        )

    got = phase((value_grad, layer_input, residual_grad, value_weight, place, low == 1, end == 1, core * half))
    value_grad, layer_input, residual_grad, value_weight, place, is_low, is_end, first_row = got

    v0 = value_grad
    w_own = lax.dynamic_slice_in_dim(value_weight, first_row, half, 0)
    in_other, res_other = core_swap(layer_input), core_swap(residual_grad)
    v0_other = core_swap(v0)
    w_inner, in_other = phase((w_own, in_other))
    turned = call(turn_kernel, jax.ShapeDtypeStruct((2, 4 * half, tokens), BF16), [], 1 << 30, layer_input, in_other)
    term0, send0 = term((v0, v0_other), (0, 4))
    w_beside = outer(w_own)
    got = phase((inner(w_inner), square(v0, 1), square(v0, 2), turned, term0, send0, res_other))
    w_mid, vx, vy, turned, term0, send0, res_other = got

    vx_other, vy_other = core_swap(vx), core_swap(vy)
    term1, send1, near1 = term((vx, vy, vx_other, vy_other), (0, 2), (2, 1))
    owner, key_row, turned = phase((owner, key_row, turned))
    key = owner[:, 0] * keys + key_row
    key_both = jnp.concatenate([key, core_swap(key)])[None, :]
    chosen = call(choose_kernel, struct(4 * keys, 2 * tokens, BF16), [], 0, key_both)
    i0 = outer(jnp.where(is_end, send0, w_mid))
    got = phase((inner(w_beside), square(v0, 3), term1, send1, near1, chosen))
    w_end, vd, term1, send1, near1, chosen = got
    w_third = i0

    vd_other, sums0 = phase((core_swap(vd), far_plus(term0, i0)))
    b0 = inner(sums0)
    term2, send2, near2 = term((vd, vd_other), (0, 2), (2, 1))
    back0 = plus(term0[2 * half : 3 * half], b0[:, :heads])
    send2 = jnp.where(is_end, send2, jnp.concatenate([back0, back0], 1))
    send_a, keep_a, send_mid, keep_mid = back(
        back_kernel, (3, 1), 1 << 30, [pltpu.VMEM((3 * half, 4 * heads), BF16)],
        w_own, w_beside, w_mid, w_third, w_end,
    )
    got = phase((outer(jnp.where(is_end, send1, w_end)), b0, term1, term2, send_a, keep_a, term0, near1, near2, send2))
    i1, b0, term1, term2, send_a, keep_a, term0, near1, near2, send2 = got
    w_fourth = i1

    def joined(a, b):
        return jnp.where(is_low, jnp.concatenate([a, b], 1), jnp.concatenate([b, a], 1))

    i2 = outer(send2)
    send_b, keep_b = back(back_end_kernel, (1,), 1 << 29, [], w_fourth, send_mid, keep_mid)
    keep = joined(keep_a, keep_b)
    b1 = inner(far_plus(term1, i1))
    b2 = inner(far_plus(term2, i2))
    got = phase((outer(joined(send_a, send_b)), b1, b2, term0, term1, term2, keep, i2))
    k1, b1, b2, term0, term1, term2, keep, i2 = got

    k2 = across(plus(keep[keys:], k1[keys:]))
    back1 = plus(term1[2 * half : 3 * half], b1[:, : 2 * heads])
    back2 = plus(term2[2 * half : 3 * half], b2[:, :heads])
    i3 = outer(jnp.where(
        is_end, jnp.concatenate([near1, near2], 1), jnp.concatenate([back1, back2], 1)
    ))
    key_half = keep[:keys] + k1[:keys].astype(F32)
    weight_half = jnp.concatenate([
        term0[3 * half :] + jnp.where(is_end, i2[:, :heads], i0[:, 2 * heads : 3 * heads]).astype(F32)
        + b0[:, heads:].astype(F32),
        term1[3 * half :] + b1[:, 2 * heads :].astype(F32),
        term2[3 * half :] + b2[:, heads:].astype(F32),
    ], 1)
    outs = (struct(part, 4 * heads, F32), struct(keys, features, F32))
    return tuple(pl.pallas_call(
        join_kernel,
        out_shape=outs,
        in_specs=[smem] + [vmem] * 8,
        out_specs=(pl.BlockSpec(memory_space=pl.ANY),) * 2,
        scratch_shapes=[pltpu.VMEM(o.shape, F32) for o in outs] + [pltpu.SemaphoreType.DMA((4,))],
        compiler_params=pltpu.CompilerParams(vmem_limit_bytes=16 << 20),
        cost_estimate=pl.CostEstimate(flops=0, bytes_accessed=1 << 20, transcendentals=0),
    )(place, weight_half, core_swap(weight_half), i3, core_swap(i3), key_half, core_swap(key_half), k2, core_swap(k2)))


def solution(mesh):
    shape = dict(mesh.shape)
    special = shape == {"dp": 2, "fsdp": 4, "tp": 4}
    return jax.shard_map(
        pair_body if special else general_body,
        mesh=mesh,
        in_specs=(
            P(("dp", "fsdp"), "tp"),
            P(("dp", "fsdp"), "tp"),
            P(("dp", "fsdp"), "tp"),
            P(("tp", "fsdp"), None),
            P(("dp", "fsdp"), None),
            P(("dp", "fsdp")),
        ),
        out_specs=(P(("tp", "fsdp"), None), P("fsdp", "tp")),
        check_vma=False,
    )
```

```python
import functools

import jax
import jax.numpy as jnp
from jax import lax
from jax.experimental import pallas as pl
from jax.experimental.pallas import tpu as pltpu
from jax.sharding import PartitionSpec as P

F32, BF16 = jnp.float32, jnp.bfloat16
KEY_DEV = 256


def dot(a, b, ca, cb):
    return lax.dot_general(a, b, (((ca,), (cb,)), ((), ())), preferred_element_type=F32)


def general_body(layer_input, value_grad, residual_grad, value_weight, owner, key_row):
    all_heads = lax.all_gather(value_grad, "tp", axis=1, tiled=True)
    tok_rows, features = layer_input.shape
    groups = lax.axis_size("fsdp")
    slots = 2 * tok_rows // groups
    keys_here = KEY_DEV
    width = all_heads.shape[1]
    term = dot(layer_input, all_heads, 0, 0)
    pieces = term.astype(BF16).reshape(groups, features // groups, width)
    arrived = lax.all_to_all(pieces, "fsdp", split_axis=0, concat_axis=0, tiled=True)
    shard = jnp.sum(arrived.astype(F32), axis=0)
    back = dot(all_heads, lax.all_gather(value_weight, "fsdp", axis=0, tiled=True), 1, 1)
    input_grad = (residual_grad.astype(F32) + back).astype(BF16)
    target = owner[:, 0]
    onehot = (target[:, None] == jnp.arange(groups, dtype=jnp.int32)[None, :]).astype(jnp.int32)
    position = jnp.sum(jnp.cumsum(onehot, axis=0) * onehot, axis=1) - 1
    place = target * slots + position
    chooser = jnp.arange(groups * slots, dtype=jnp.int32)[:, None] == place[None, :]
    outgoing = dot(chooser.astype(BF16), input_grad, 1, 0).astype(BF16)
    out_keys = jnp.sum(jnp.where(chooser, key_row[None, :] + 1, 0), axis=1) - 1
    arrived = lax.all_to_all(outgoing, "fsdp", split_axis=0, concat_axis=0, tiled=True)
    arrived_keys = lax.all_to_all(out_keys, "fsdp", split_axis=0, concat_axis=0, tiled=True)
    selector = (arrived_keys[:, None] == jnp.arange(keys_here, dtype=jnp.int32)[None, :]).astype(BF16)
    table = dot(selector, arrived, 0, 0)
    return lax.psum(shard, "dp"), lax.psum(table, "dp")


def turn_kernel(place, mine, other, out):
    half = mine.shape[1] // 8
    for side, ref in enumerate((mine, other)):
        for i, rank in enumerate((8, 7, 6, 5)):
            cols = pl.ds(pl.multiple_of((2 * place[rank] + place[4]) * half, half), half)
            out[side, i * half : (i + 1) * half, :] = ref[:, cols].T


def term_kernel(rounded, place, turned, *refs):
    n = sum(r.shape == refs[0].shape for r in refs) // 2
    heads, out, sends = refs[: 2 * n], refs[2 * n], refs[1 + 2 * n :]
    width = heads[0].shape[1]
    for k in range(n):
        cols = slice(k * width, (k + 1) * width)
        out[:, cols] = dot(turned[0], heads[k][...], 1, 0) + dot(turned[1], heads[n + k][...], 1, 0)
    half, wide = out.shape[0] // 4, out.shape[1]
    for first, send in zip(rounded, sends):
        for j in range(send.shape[1] // wide):
            row = (first + j) * half
            send[:, j * wide : (j + 1) * wide] = out[row : row + half, :].astype(BF16)


def choose_kernel(place, key, out):
    keys = out.shape[0] // 4
    row = lax.broadcasted_iota(jnp.int32, (keys, key.shape[1]), 0)
    for j in range(4):
        hit = row + place[10 + j] * keys == key[...]
        out[j * keys : (j + 1) * keys, :] = jnp.where(hit, 1.0, 0.0).astype(BF16)


def back_rows(place, first, count, weight, residuals, heads, chosen, send, keep):
    half = weight.shape[0] // count
    tokens, width = heads[0].shape
    total = [None] * 2
    starts = [pl.multiple_of((2 * (first + p) + place[4]) * half, half) for p in range(count)]
    for side in range(2):
        acc = jnp.concatenate([residuals[side][:, pl.ds(at, half)] for at in starts], 1).astype(F32)
        for k in range(4):
            cols = pl.ds(pl.multiple_of(place[k] * width, width), width)
            acc = acc + dot(heads[4 * side + k][...], weight[:, cols], 1, 1)
        rows = acc.astype(BF16)
        for i in range(2):
            size = send.shape[0]
            pick = chosen[i * size : (i + 1) * size, side * tokens : (side + 1) * tokens]
            add = dot(pick, rows, 1, 0)
            total[i] = add if side == 0 else total[i] + add
    send[...] = total[0].astype(BF16)
    keep[...] = total[1]


def back_kernel(place, *refs):
    residuals, heads, chosen, refs = refs[:2], refs[2:10], refs[10], refs[11:]
    own, beside, mid, third, end, send, keep, send_mid, keep_mid, weight = refs
    half = own.shape[0]
    first = place[14]

    def put(rank, ref):
        weight[pl.ds(pl.multiple_of((place[rank] - first) * half, half), half), :] = ref[...]

    put(5, own)
    put(6, beside)
    pl.when(place[9] == 0)(lambda: put(7, mid))
    pl.when(place[9] == 1)(lambda: put(7, third))
    back_rows(place, first, 3, weight, residuals, heads, chosen, send, keep)
    pl.when(place[9] == 0)(
        lambda: back_rows(place, place[8], 1, end, residuals, heads, chosen, send_mid, keep_mid)
    )


def back_end_kernel(place, *refs):
    residuals, heads, chosen, (fourth, send_mid, keep_mid, send, keep) = refs[:2], refs[2:10], refs[10], refs[11:]

    @pl.when(place[9] == 0)
    def _():
        send[...] = send_mid[...]
        keep[...] = keep_mid[...]

    pl.when(place[9] == 1)(lambda: back_rows(place, place[8], 1, fourth, residuals, heads, chosen, send, keep))


def join_kernel(place, mine, pair, last, last_pair, key_mine, key_pair, key_last, key_last_pair,
                out, key_out, joined, key_joined, sems):
    half, width = mine.shape[0], mine.shape[1] // 4
    copies = []
    for side in range(2):
        here = place[4] == side
        rows = pl.ds(side * half, half)
        for k in range(4):
            cols = slice(k * width, (k + 1) * width)
            value = jnp.where(here, mine[:, cols], pair[:, cols])
            if k > 0:
                came = slice((k - 1) * width, k * width)
                value = value + jnp.where(here, last[:, came], last_pair[:, came]).astype(F32)
            joined[rows, pl.ds(pl.multiple_of(place[k] * width, width), width)] = value
        copies.append(pltpu.make_async_copy(joined.at[rows], out.at[rows], sems.at[side]))
        copies[-1].start()
    size, high = key_mine.shape[1] // 4, key_mine.shape[0] // 2
    first = place[4] == 0
    for part in range(2):
        rows = pl.ds(part * high, high)
        for p in range(4):
            cols = slice(p * size, (p + 1) * size)
            a = key_mine[rows, cols] + key_last[rows, cols].astype(F32)
            b = key_pair[rows, cols] + key_last_pair[rows, cols].astype(F32)
            key_joined[rows, 2 * p * size : (2 * p + 1) * size] = jnp.where(first, a, b)
            key_joined[rows, (2 * p + 1) * size : (2 * p + 2) * size] = jnp.where(first, b, a)
        copies.append(pltpu.make_async_copy(key_joined.at[rows], key_out.at[rows], sems.at[2 + part]))
        copies[-1].start()
    for copy in copies:
        copy.wait()


def pair_body(layer_input, value_grad, residual_grad, value_weight, owner, key_row):
    core, z, t = (lax.axis_index(n) for n in ("dp", "fsdp", "tp"))
    tokens, features = layer_input.shape
    heads = value_grad.shape[1]
    part = features // 4
    half = part // 2
    keys = KEY_DEV
    phase = lax.optimization_barrier

    def core_swap(v):
        return lax.ppermute(v, "dp", [(0, 1), (1, 0)])

    def outer(v):
        return lax.ppermute(v, "fsdp", [(0, 1), (1, 0), (2, 3), (3, 2)])

    def inward(v):
        return lax.ppermute(v, "fsdp", [(0, 1), (3, 2)])

    def outward(v):
        return lax.ppermute(v, "fsdp", [(1, 0), (2, 3)])

    def inner(v):
        return lax.ppermute(v, "fsdp", [(1, 2), (2, 1)])

    end = ((z == 0) | (z == 3)).astype(jnp.int32)
    low = (z < 2).astype(jnp.int32)
    beside = z ^ 1
    far_mid = 1 + low
    far_end = 3 * low
    place = jnp.stack([t, t ^ 1, t ^ 2, t ^ 3, core, z, beside, far_mid, far_end, end, z ^ 1, z ^ 3, z, z ^ 2, 1 - low]).astype(jnp.int32)
    smem, vmem = pl.BlockSpec(memory_space=pltpu.SMEM), pl.BlockSpec(memory_space=pltpu.VMEM)

    def call(kernel, out, scratch, flops, *args):
        return pl.pallas_call(
            kernel,
            out_shape=out,
            in_specs=[smem] + [vmem] * len(args),
            out_specs=jax.tree.map(lambda o: vmem, out),
            scratch_shapes=scratch,
            compiler_params=pltpu.CompilerParams(vmem_limit_bytes=16 << 20),
            cost_estimate=pl.CostEstimate(flops=flops, bytes_accessed=(1 << 20) if flops else 0, transcendentals=0),
        )(place, *args)

    def square(v, d):
        return lax.ppermute(v, "tp", [(i, i ^ d) for i in range(4)])

    def across(v):
        return lax.ppermute(v, "fsdp", [(i, i ^ 2) for i in range(4)])

    def struct(rows, cols, dtype):
        return jax.ShapeDtypeStruct((rows, cols), dtype)

    def term(v, *parts):
        n = len(v) // 2 * heads
        out = (struct(4 * half, n, F32),) + tuple(struct(half, count * n, BF16) for _, count in parts)
        kernel = functools.partial(term_kernel, tuple(first for first, _ in parts))
        return call(kernel, out, [], (2 << 30) if len(v) == len(parts) == 2 else 0, turned, *v)

    def plus(v, came):
        return (v + came.astype(F32)).astype(BF16)

    def far_plus(v, came):
        n = v.shape[1]
        return jnp.concatenate([plus(v[:half], came[:, :n]), plus(v[half : 2 * half], came[:, n : 2 * n])], 1)

    def back(kernel, parts, cost, scratch, *refs):
        out = [struct(2 * keys, n * half, kind) for n in parts for kind in (BF16, F32)]
        return call(
            kernel, out, scratch, cost, residual_grad, res_other,
            v0, vx, vy, vd, v0_other, vx_other, vy_other, vd_other, chosen, *refs,
        )

    got = phase((value_grad, layer_input, residual_grad, value_weight, place, low == 1, end == 1, core * half))
    value_grad, layer_input, residual_grad, value_weight, place, is_low, is_end, first_row = got

    v0 = value_grad
    w_own = lax.dynamic_slice_in_dim(value_weight, first_row, half, 0)
    in_other, res_other = core_swap(layer_input), core_swap(residual_grad)
    v0_other = core_swap(v0)
    w_inner, in_other = phase((w_own, in_other))
    turned = call(turn_kernel, jax.ShapeDtypeStruct((2, 4 * half, tokens), BF16), [], 1 << 30, layer_input, in_other)
    term0, send0 = term((v0, v0_other), (0, 4))
    w_beside = outer(w_own)
    got = phase((inner(w_inner), square(v0, 1), square(v0, 2), turned, term0, send0, res_other))
    w_mid, vx, vy, turned, term0, send0, res_other = got

    vx_other, vy_other = core_swap(vx), core_swap(vy)
    term1, send1, near1 = term((vx, vy, vx_other, vy_other), (0, 2), (2, 1))
    owner, key_row, turned = phase((owner, key_row, turned))
    key = owner[:, 0] * keys + key_row
    key_both = jnp.concatenate([key, core_swap(key)])[None, :]
    chosen = call(choose_kernel, struct(4 * keys, 2 * tokens, BF16), [], 0, key_both)
    i0 = outer(jnp.where(is_end, send0, w_mid))
    got = phase((inner(w_beside), square(v0, 3), term1, send1, near1, chosen))
    w_end, vd, term1, send1, near1, chosen = got
    w_third = i0

    vd_other, sums0 = phase((core_swap(vd), far_plus(term0, i0)))
    b0 = inner(sums0)
    term2, send2, near2 = term((vd, vd_other), (0, 2), (2, 1))
    back0 = plus(term0[2 * half : 3 * half], b0[:, :heads])
    send2 = jnp.where(is_end, send2, jnp.concatenate([back0, back0], 1))
    send_a, keep_a, send_mid, keep_mid = back(
        back_kernel, (3, 1), 1 << 30, [pltpu.VMEM((3 * half, 4 * heads), BF16)],
        w_own, w_beside, w_mid, w_third, w_end,
    )
    got = phase((outer(jnp.where(is_end, send1, w_end)), b0, term1, term2, send_a, keep_a, term0, near1, near2, send2))
    i1, b0, term1, term2, send_a, keep_a, term0, near1, near2, send2 = got
    w_fourth = i1

    def joined(a, b):
        return jnp.where(is_low, jnp.concatenate([a, b], 1), jnp.concatenate([b, a], 1))

    i2 = outer(send2)
    send_b, keep_b = back(back_end_kernel, (1,), 1 << 29, [], w_fourth, send_mid, keep_mid)
    keep = joined(keep_a, keep_b)
    b1 = inner(far_plus(term1, i1))
    b2 = inner(far_plus(term2, i2))
    k1, b1, keep, i2, term0 = phase((outer(joined(send_a, send_b)), b1, keep, i2, term0))

    k2 = across(plus(keep[keys:], k1[keys:]))
    back1 = plus(term1[2 * half : 3 * half], b1[:, : 2 * heads])
    back2 = plus(term2[2 * half : 3 * half], b2[:, :heads])
    i3 = outer(jnp.where(
        is_end, jnp.concatenate([near1, near2], 1), jnp.concatenate([back1, back2], 1)
    ))
    key_half = keep[:keys] + k1[:keys].astype(F32)
    weight_half = jnp.concatenate([
        term0[3 * half :] + jnp.where(is_end, i2[:, :heads], i0[:, 2 * heads : 3 * heads]).astype(F32)
        + b0[:, heads:].astype(F32),
        term1[3 * half :] + b1[:, 2 * heads :].astype(F32),
        term2[3 * half :] + b2[:, heads:].astype(F32),
    ], 1)
    outs = (struct(part, 4 * heads, F32), struct(keys, features, F32))
    return tuple(pl.pallas_call(
        join_kernel,
        out_shape=outs,
        in_specs=[smem] + [vmem] * 8,
        out_specs=(pl.BlockSpec(memory_space=pl.ANY),) * 2,
        scratch_shapes=[pltpu.VMEM(o.shape, F32) for o in outs] + [pltpu.SemaphoreType.DMA((4,))],
        compiler_params=pltpu.CompilerParams(vmem_limit_bytes=16 << 20),
        cost_estimate=pl.CostEstimate(flops=0, bytes_accessed=1 << 20, transcendentals=0),
    )(place, weight_half, core_swap(weight_half), i3, core_swap(i3), key_half, core_swap(key_half), k2, core_swap(k2)))


def solution(mesh):
    shape = dict(mesh.shape)
    special = shape == {"dp": 2, "fsdp": 4, "tp": 4}
    return jax.shard_map(
        pair_body if special else general_body,
        mesh=mesh,
        in_specs=(
            P(("dp", "fsdp"), "tp"),
            P(("dp", "fsdp"), "tp"),
            P(("dp", "fsdp"), "tp"),
            P(("tp", "fsdp"), None),
            P(("dp", "fsdp"), None),
            P(("dp", "fsdp")),
        ),
        out_specs=(P(("tp", "fsdp"), None), P("fsdp", "tp")),
        check_vma=False,
    )
```
